128 devices in a mesh: dp: 4 (over x), expert: 32 (over z, y, core).
Axes of the slice: x: 4, y: 4, z: 4, core: 2. Of those that a mesh axis runs over, the one named last changes fastest.
Arguments:
- tokens: bfloat16 [16384, 2048], P(('dp', 'expert')), may hold values from -6 to 6
- expert_ids: int32 [16384, 8], P(('dp', 'expert')), may hold values from 0 to 63, all different within a row; in each aligned block of 128 rows (0 to 127, 128 to 255, ...) at most 18 rows name the same one
- gate_logits: float32 [16384, 8], P(('dp', 'expert')), may hold values from -400 to 400
- upstream: bfloat16 [16384, 2048], P(('dp', 'expert')), may hold values from -6 to 6
- w_gate: bfloat16 [64, 2048, 768], P('expert'), may hold values from -0.125 to 0.125
- w_up: bfloat16 [64, 2048, 768], P('expert'), may hold values from -0.125 to 0.125
- w_down: bfloat16 [64, 768, 2048], P('expert'), may hold values from -0.21875 to 0.21875
Outputs:
- grad_tokens: bfloat16 [16384, 2048], P(('dp', 'expert'))
- grad_logits: float32 [16384, 8], P(('dp', 'expert'))
- grad_gate: bfloat16 [64, 2048, 768], P('expert', 'dp')
- grad_up: bfloat16 [64, 2048, 768], P('expert', 'dp')
- grad_down: bfloat16 [64, 768, 2048], P('expert', None, 'dp')
The draws below stay inside these ranges and needn't reach their ends.
Inputs may be any that keep to these rules, and one draw needn't show every extreme that they name: `expert_ids`: each row names 8 different experts. Among the 128 rows of one device no expert is named more than 18 times; in some device's rows one expert is named exactly 18 times.
All inputs are finite; a program needn't handle non-finite values.
Results may differ from the reference program's by a relative error of at most 0.013.
Values may be sent and summed in bfloat16 or wider, within the bound.
A program may use at most 192 MiB of HBM per device.

```python
import math
import jax
import jax.numpy as jnp
import numpy as np
from jax import lax

D = 2048
FF = 768
TOP = 8
ROWS_DEV = 128
EXPERTS = 64
CAP = 18
TOKENS = 16384
N_DP = 4
N_EXPERT = 32


def draw_gate_logits(key, part):
    key = jax.random.fold_in(key, 7)
    base_key = jax.random.fold_in(key, 0)
    offset_key = jax.random.fold_in(key, 3)
    spread = jnp.clip(0.25 * jax.random.normal(base_key, (TOKENS, TOP), jnp.float32), -0.5, 0.5)
    offset = jnp.clip(2.0 * jax.random.normal(offset_key, (TOKENS, 1), jnp.float32), -6.0, 6.0)
    logits = spread + offset
    return logits


def level_of(key, dims, cuts, smallest, high):
    factor_of, own = 1.0, jax.random.fold_in(key, 6)
    for dim, parts in cuts:
        steps = jnp.exp(jax.random.uniform(jax.random.fold_in(own, dim), (parts,), jnp.float32, smallest / len(cuts), high / len(cuts)))
        factor_of = factor_of * jnp.repeat(steps, dims[dim] // parts).reshape([-1 if axis == dim else 1 for axis in range(len(dims))])
    return factor_of


def assign_block(stream_key, own, number, rows, number_of, top, most, slope):
    order = jax.random.permutation(stream_key, number_of)
    crowded, ordinary = portions_of(number_of, rows * top, most, slope, True), portions_of(number_of, rows * top, most, slope, False)
    places = jnp.arange(number_of)

    def named(lengths, offset_by):
        used = int((lengths > 0).sum())
        fixed = max(1, used // 4)
        shifted = fixed + (places - fixed + offset_by * (used - fixed)) % max(1, number_of - fixed)
        return jnp.zeros((number_of,), jnp.int32).at[order[jnp.where(places < fixed, places, shifted)]].set(jnp.asarray(lengths, jnp.int32))

    lengths = jnp.where(number % 4 == 0, named(crowded, number // 4), named(ordinary, number - number // 4 - 1))
    mixed = jax.random.permutation(jax.random.fold_in(own, 3), number_of)
    source_of, receiver = mixed[0:number_of // 2 * 2:2], mixed[1:number_of // 2 * 2:2]
    slack = jnp.minimum(lengths[source_of] - 1, most - lengths[receiver]) // 2
    slack = jnp.where((source_of == order[0]) | (receiver == order[0]) | (lengths[receiver] == 0), 0, jnp.maximum(slack, 0))
    shifted = jax.random.randint(jax.random.fold_in(own, 4), (number_of // 2,), 0, 1 << 20) % (slack + 1)
    lengths = lengths.at[source_of].add(-shifted).at[receiver].add(shifted)
    members = jnp.searchsorted(jnp.cumsum(lengths), jnp.arange(rows * top), side="right").astype(jnp.int32)
    table = members.reshape(top, rows).T
    table = table[jax.random.permutation(jax.random.fold_in(own, 1), rows)]
    offset_by = jax.random.randint(jax.random.fold_in(own, 2), (rows, 1), 0, top)
    return jnp.take_along_axis(table, (jnp.arange(top)[None, :] + offset_by) % top, axis=1)


def portions_of(amount, total, most, slope, full):
    weights = [(1 << 20) // math.isqrt(rank ** slope) + 1 for rank in range(1, amount + 1)]
    largest = most if full else min(most, max(-(-total // amount), total * weights[0] // sum(weights)))
    least = 1 if total - largest >= amount - 1 else 0
    counts, surplus = [largest] + [least] * (amount - 1), total - largest - least * (amount - 1)
    while surplus > 0:
        movable = [i for i in range(1, amount) if counts[i] < largest] or [i for i in range(1, amount) if counts[i] < most]
        whole, remaining = sum([weights[i] for i in movable]), surplus
        for i in movable:
            extra = min(most - counts[i], max(1, remaining * weights[i] // whole), surplus)
            counts[i] = counts[i] + extra
            surplus = surplus - extra
    return np.array(counts)


def normal_values(rng, shape, scale, most, shards=(), held_as=jnp.bfloat16):
    gain = level_of(rng, shape, shards, -0.22, 0.18) if shards else 1.0
    entries = jax.random.normal(rng, shape, jnp.float32) * scale * gain
    return jnp.minimum(jnp.maximum(entries, -most), most).astype(held_as)


def setup_inputs(seed: int = 0) -> dict:
    seeds = jax.random.split(jax.random.key(seed), 8)
    tokens = normal_values(seeds[0], (TOKENS, D), 1.0, 6.0, ((0, 128),))
    expert_ids_keys = jax.random.split(jax.random.fold_in(seeds[1], 1), TOKENS // ROWS_DEV)
    expert_ids_turns = jax.random.permutation(jax.random.fold_in(seeds[1], 3), TOKENS // ROWS_DEV)
    expert_ids = jax.vmap(lambda own, number: assign_block(jax.random.fold_in(seeds[1], 2), own, number, ROWS_DEV, EXPERTS, TOP, CAP, 2))(expert_ids_keys, expert_ids_turns).reshape((TOKENS, TOP))
    gate_logits = draw_gate_logits(jax.random.fold_in(seeds[7], 71), 0)
    upstream = normal_values(seeds[3], (TOKENS, D), 1.0, 6.0, ((0, 128),))
    w_gate = normal_values(seeds[4], (EXPERTS, D, FF), D ** -0.5, 0.125, ((0, 32),))
    w_up = normal_values(seeds[5], (EXPERTS, D, FF), D ** -0.5, 0.125, ((0, 32),))
    w_down = normal_values(seeds[6], (EXPERTS, FF, D), FF ** -0.5, 0.21875, ((0, 32),))
    return dict(tokens=tokens, expert_ids=expert_ids, gate_logits=gate_logits, upstream=upstream, w_gate=w_gate, w_up=w_up, w_down=w_down)


def reduce_groups(partial_sum):
    rounded = lax.optimization_barrier(partial_sum.astype(jnp.bfloat16))
    return jnp.sum(rounded.astype(jnp.float32), axis=0).astype(jnp.bfloat16)


def reference(tokens, expert_ids, gate_logits, upstream, w_gate, w_up, w_down):
    assign_count = TOKENS * TOP
    slot_width = N_EXPERT * CAP
    block_count = TOKENS // ROWS_DEV
    gate_probs = jax.nn.softmax(gate_logits.astype(jnp.float32), axis=-1)
    gate_rounded = gate_probs.astype(jnp.bfloat16)
    flat_expert = expert_ids.reshape(-1).astype(jnp.int32)
    one_hot = (flat_expert.reshape(block_count, ROWS_DEV * TOP)[:, :, None]
               == jnp.arange(EXPERTS, dtype=jnp.int32)[None, None, :]).astype(jnp.int32)
    slot_rank = jnp.sum((jnp.cumsum(one_hot, axis=1) - one_hot) * one_hot, axis=-1).reshape(-1)
    assign_ids = jnp.arange(assign_count, dtype=jnp.int32)
    block_ids = assign_ids // (ROWS_DEV * TOP)
    group_ids = block_ids // N_EXPERT
    source_ids = block_ids % N_EXPERT
    slot_pos = ((group_ids * EXPERTS + flat_expert) * N_EXPERT + source_ids) * CAP + slot_rank
    slot_table = jnp.full((N_DP * EXPERTS * slot_width,), assign_count, jnp.int32)
    slot_table = slot_table.at[slot_pos].set(assign_ids)
    slot_table = slot_table.reshape(N_DP, EXPERTS, slot_width).transpose(1, 0, 2)
    tokens_padded = jnp.concatenate([tokens, jnp.zeros((1, D), jnp.bfloat16)], axis=0)
    upstream_padded = jnp.concatenate([upstream, jnp.zeros((1, D), jnp.bfloat16)], axis=0)
    gates_padded = jnp.concatenate([gate_rounded.reshape(-1), jnp.zeros((1,), jnp.bfloat16)], axis=0)

    def per_expert(carry, items):
        dx_total, dgate_total = carry
        table_slice, gate_weight, up_weight, down_weight = items
        slot_ids = table_slice.reshape(-1)
        token_ids = jnp.where(slot_ids < assign_count, slot_ids // TOP, TOKENS).astype(jnp.int32)
        token_rows = tokens_padded[token_ids]
        grad_rows = upstream_padded[token_ids]
        gate_column = gates_padded[slot_ids].astype(jnp.float32)[:, None]
        pre_gate = jnp.dot(token_rows, gate_weight, preferred_element_type=jnp.float32)
        pre_up = jnp.dot(token_rows, up_weight, preferred_element_type=jnp.float32)
        sigmoid_gate = jax.nn.sigmoid(pre_gate)
        activated = pre_gate * sigmoid_gate
        hidden = activated * pre_up
        raw_grad = jnp.dot(grad_rows, down_weight.T, preferred_element_type=jnp.float32)
        slot_dgate = jnp.sum(raw_grad * hidden, axis=-1)
        d_hidden = gate_column * raw_grad
        d_pre_gate = (d_hidden * pre_up * sigmoid_gate * (1.0 + pre_gate * (1.0 - sigmoid_gate))).astype(jnp.bfloat16)
        d_pre_up = (d_hidden * activated).astype(jnp.bfloat16)
        weighted_hidden = (gate_column * hidden).astype(jnp.bfloat16)
        slot_dx = (jnp.dot(d_pre_gate, gate_weight.T, preferred_element_type=jnp.float32)
                   + jnp.dot(d_pre_up, up_weight.T, preferred_element_type=jnp.float32)).astype(jnp.bfloat16)
        rows_f = token_rows.astype(jnp.float32).reshape(N_DP, slot_width, D)
        grads_f = grad_rows.astype(jnp.float32).reshape(N_DP, slot_width, D)
        gate_grad = reduce_groups(jnp.einsum("gmd,gmf->gdf", rows_f, d_pre_gate.astype(jnp.float32).reshape(N_DP, slot_width, FF)))
        up_grad = reduce_groups(jnp.einsum("gmd,gmf->gdf", rows_f, d_pre_up.astype(jnp.float32).reshape(N_DP, slot_width, FF)))
        down_grad = reduce_groups(jnp.einsum("gmf,gmd->gfd", weighted_hidden.astype(jnp.float32).reshape(N_DP, slot_width, FF), grads_f))
        dx_total = dx_total.at[token_ids].add(slot_dx.astype(jnp.float32))
        dgate_round = lax.optimization_barrier(slot_dgate.astype(jnp.bfloat16))
        dgate_total = dgate_total.at[slot_ids].set(dgate_round.astype(jnp.float32))
        return (dx_total, dgate_total), (gate_grad, up_grad, down_grad)

    start = (jnp.zeros((TOKENS + 1, D), jnp.float32), jnp.zeros((assign_count + 1,), jnp.float32))
    final, stacked = lax.scan(per_expert, start, (slot_table, w_gate, w_up, w_down))
    dx_total, dgate_total = final
    grad_tokens = dx_total[:TOKENS].astype(jnp.bfloat16)
    dgate_rows = dgate_total[:assign_count].reshape(TOKENS, TOP)
    grad_logits = gate_probs * (dgate_rows - jnp.sum(gate_probs * dgate_rows, axis=-1, keepdims=True))
    return grad_tokens, grad_logits, stacked[0], stacked[1], stacked[2]
```

```python
import jax
import jax.numpy as jnp
from jax import lax
from jax.experimental import pallas as pl
from jax.experimental.pallas import tpu as pltpu
from jax.sharding import PartitionSpec as P

MESH = pl.DeviceIdType.MESH
BF = jnp.bfloat16
F32 = jnp.float32
D, FF, NE, NX = 2048, 768, 32, 4
MAIN, OVF = 16, 2
ROWS = NE * (MAIN + OVF)
BACK = D + 256 + 128
ANY = pl.BlockSpec(memory_space=pl.ANY)
VMEM = pl.BlockSpec(memory_space=pltpu.VMEM)


def iota(shape, dim):
    return lax.broadcasted_iota(jnp.int32, shape, dim)


def dot_nt(a, b):
    return lax.dot_general(a, b, (((1,), (1,)), ((), ())), preferred_element_type=F32)


def dot_tn(a, b):
    return lax.dot_general(a, b, (((0,), (0,)), ((), ())), preferred_element_type=F32)


def dot(a, b):
    return jnp.dot(a, b, preferred_element_type=F32)


def routing_table(ids, gate_rounded):
    expert = iota((128, 64), 1)
    routed = jnp.zeros((128, 64), F32)
    gates = jnp.zeros((128, 64), F32)
    for k in range(8):
        hit = ids[:, k : k + 1] == expert
        routed = routed + jnp.where(hit, 1.0, 0.0)
        gates = gates + jnp.where(hit, gate_rounded[:, k : k + 1], 0.0)
    before = jnp.where(iota((128, 128), 1) < iota((128, 128), 0), 1.0, 0.0)
    rank = dot(before.astype(BF), routed.astype(BF))
    return jnp.concatenate([jnp.where(routed > 0, rank + 1.0, 0.0), gates], axis=1).astype(BF)


def slot_targets():
    row, lane = iota((80, 256), 0), iota((80, 256), 1)
    over = row - 64
    core = jnp.where(row < 64, (row % 32) // 16, (over % 4) // 2)
    slot = jnp.where(row < 64, row % 16, 16 + over % 2)
    ok = (core == lane // 128) & (row < 72)
    second = ((row >= 32) & (row < 64)) | (over >= 4)
    return jnp.where(ok, slot + 1, -1).astype(F32), jnp.where(second, 1.0, 0.0)


def kernel(
    tg, ug, wg, wu, wd, tab, ids, probs,
    gtok, glog, gg, gu, gd, rb, back,
    stage, pmat, xs, us, ov, xgate, wgv, wuv, wdv, pre_g, pre_u, wh, dgu, dgacc,
    sa, ra, sb, rbv, own, outv, outd, dxs, bkv, tokacc,
    stage_sem, w_sem, sa_s, ra_r, sb_s, rb_r, bk_s, bk_r, ld_sem, out_sem,
):
    x, me = lax.axis_index("dp"), lax.axis_index("expert")
    right, left = lax.rem(x + 1, NX), lax.rem(x + 3, NX)

    barrier = pltpu.get_barrier_semaphore()

    def greet(i, c):
        pl.semaphore_signal(barrier, inc=1, device_id=(x, lax.rem(me + i, NE)), device_id_type=MESH)
        return c

    lax.fori_loop(1, NE, greet, 0)
    for other in (right, left):
        pl.semaphore_signal(barrier, inc=1, device_id=(other, me), device_id_type=MESH)

    def wload(e):
        return [
            pltpu.make_async_copy(wg.at[e], wgv, w_sem.at[0]),
            pltpu.make_async_copy(wu.at[e], wuv, w_sem.at[1]),
        ]

    def wdload(e):
        return pltpu.make_async_copy(wd.at[e], wdv, w_sem.at[2])

    def start_weights(e):
        for cp in wload(e):
            cp.start()

    start_weights(0)
    wdload(0).start()

    target, second = slot_targets()

    def dispatch(src, dst, table):
        w = src.shape[2]

        def load(j, slot):
            return pltpu.make_async_copy(src.at[j], stage.at[slot, :, pl.ds(0, w)], stage_sem.at[slot])

        load(0, 0).start()

        def body(j, c):
            slot = lax.rem(j, 2)

            @pl.when(j + 1 < 16)
            def _():
                load(j + 1, 1 - slot).start()

            load(j, slot).wait()
            if table:
                tabj = stage[slot, :, D : D + 128]
                pick = jnp.where(iota((8, 128), 1) == 2 * me + iota((8, 128), 0), 1.0, 0.0).astype(BF)
                ranks = dot_nt(pick, tabj)
                row0 = jnp.broadcast_to(ranks[0:1, :], (80, 256))
                row1 = jnp.broadcast_to(ranks[1:2, :], (80, 256))
                pm = jnp.where(jnp.where(second > 0.5, row1, row0) == target, 1.0, 0.0).astype(BF)
                pmat[j] = pm
                got = dot(pm, tabj)
                at = pl.multiple_of(32 * j, 32)
                xgate[0, pl.ds(at, 32), :] = got[0:32]
                xgate[1, pl.ds(at, 32), :] = got[32:64]
                ov[pl.ds(pl.multiple_of(8 * j, 8), 8), D : D + 128] = got[64:72]
            pm = pmat[j]
            for n in range(D // 512):
                cols = slice(512 * n, 512 * n + 512)
                got = dot(pm, stage[slot, :, cols])
                at = pl.multiple_of(32 * j, 32)
                dst[0, pl.ds(at, 32), cols] = got[0:32].astype(BF)
                dst[1, pl.ds(at, 32), cols] = got[32:64].astype(BF)
                ov[pl.ds(pl.multiple_of(8 * j, 8), 8), cols] = got[64:72]
            return c

        lax.fori_loop(0, 16, body, 0)
        r, col = iota((64, 128), 0), iota((64, 128), 1)
        for e in range(2):
            sel = jnp.where(col == 8 * (r // 4) + 4 * e + r % 4, 1.0, 0.0).astype(BF)
            for n in range(D // 512):
                cols = slice(512 * n, 512 * n + 512)
                dst[e, 512:576, cols] = dot(sel, ov[:, cols].astype(BF)).astype(BF)
            if table:
                xgate[e, 512:576, :] = dot(sel, ov[:, D : D + 128].astype(BF))

    dispatch(tg, xs, True)
    pl.semaphore_wait(barrier, NE - 1 + 2)

    def gate_of(e, rows):
        lane = iota((rows.size, 128), 1)
        return jnp.sum(jnp.where(lane == 64 + 2 * me + e, xgate[e, rows, :], 0.0), axis=1, keepdims=True)

    def forward(e):
        for cp in wload(e):
            cp.wait()

        def body(i, c):
            rows = pl.ds(pl.multiple_of((i // 3) * 192, 192), 192)
            cols = pl.ds(pl.multiple_of((i % 3) * 256, 256), 256)
            pg = dot(xs[e, rows, :], wgv[:, cols])
            pu = dot(xs[e, rows, :], wuv[:, cols])
            pre_g[e, rows, cols] = pg
            pre_u[e, rows, cols] = pu
            hidden = pg * jax.nn.sigmoid(pg) * pu
            wh[e, rows, cols] = (gate_of(e, rows) * hidden).astype(BF)
            return c

        lax.fori_loop(0, 9, body, 0)

    def backward(e):
        wdload(e).wait()

        def body(i, c):
            rows = pl.ds(pl.multiple_of((i // 3) * 192, 192), 192)
            cols = pl.ds(pl.multiple_of((i % 3) * 256, 256), 256)
            raw = dot_nt(us[e, rows, :], wdv[cols, :])
            pg, pu = pre_g[e, rows, cols], pre_u[e, rows, cols]
            s = jax.nn.sigmoid(pg)
            act = pg * s
            part = raw * (act * pu)
            part = part[:, 0:128] + part[:, 128:256]
            dgacc[e, rows, :] = jnp.where(i % 3 == 0, jnp.zeros_like(part), dgacc[e, rows, :]) + part
            dh = gate_of(e, rows) * raw
            dgu[e, 0, rows, cols] = (dh * pu * s * (1.0 + pg * (1.0 - s))).astype(BF)
            dgu[e, 1, rows, cols] = (dh * act).astype(BF)
            return c

        lax.fori_loop(0, 9, body, 0)
        if e == 0:
            wdload(1).start()

    def input_grad(e):
        for cp in wload(e):
            cp.wait()

        def body(i, c):
            rows = pl.ds(pl.multiple_of((i // 4) * 192, 192), 192)
            cols = pl.ds(pl.multiple_of((i % 4) * 512, 512), 512)
            dx = dot_nt(dgu[e, 0, rows, :], wgv[cols, :]) + dot_nt(dgu[e, 1, rows, :], wuv[cols, :])
            dxs[e, rows, cols] = dx.astype(BF)
            return c

        lax.fori_loop(0, 12, body, 0)
        r, col = iota((512, 64), 0), iota((512, 64), 1)
        place = 2 * (r // 16) + (r % 16) // 8 == col
        packed = jnp.zeros((512, 256), F32)
        for q in range(8):
            sel = jnp.where(place & (r % 8 == q), 1.0, 0.0).astype(BF)
            packed = packed + dot(sel, dxs[e, 512:576, 256 * q : 256 * q + 256])
        dxs[e, 0:512, D : D + 256] = packed.astype(BF)
        dgate = jnp.sum(dgacc[e], axis=1, keepdims=True).astype(BF).astype(F32)
        first = iota((512, 128), 1) == 0
        sel = jnp.where(place & (r % 8 == 0), 1.0, 0.0).astype(BF)
        over = dot(sel, jnp.broadcast_to(dgate[512:576], (64, 128)).astype(BF))
        main = jnp.broadcast_to(dgate[0:512], (512, 128))
        dxs[e, 0:512, D + 256 :] = jnp.where(first, main, over).astype(BF)

    def send_back(e):
        pltpu.make_async_copy(dxs.at[e, pl.ds(pl.multiple_of(16 * me, 16), 16)], back.at[e, me], ld_sem.at[2]).start()

        def body(i, c):
            p = lax.rem(me + i, NE)
            pltpu.make_async_remote_copy(
                src_ref=dxs.at[e, pl.ds(pl.multiple_of(16 * p, 16), 16)],
                dst_ref=back.at[e, me],
                send_sem=bk_s.at[e],
                recv_sem=bk_r.at[e],
                device_id=(x, p),
                device_id_type=MESH,
            ).start()
            return c

        lax.fori_loop(1, NE, body, 0)
        pltpu.make_async_copy(dxs.at[e, pl.ds(pl.multiple_of(16 * me, 16), 16)], back.at[e, me], ld_sem.at[2]).wait()

    def wait_back(e):
        part = back.at[e, pl.ds(0, NE - 1)]
        pltpu.make_async_copy(part, part, bk_s.at[e]).wait()
        pltpu.make_async_copy(part, part, bk_r.at[e]).wait()

    chunks = [("d", 0), ("d", 1), ("g", 0), ("u", 0), ("g", 1), ("u", 1)]

    def partial(m, quarter, put):
        kind, e = chunks[m]

        def body(i, c):
            rows = pl.ds(pl.multiple_of(i * 256, 256), 256)
            cols = pl.ds(pl.multiple_of(quarter * 512 + i * 256, 256), 256)
            a = (us if kind == "d" else xs)[e, :, cols]
            b = wh[e] if kind == "d" else dgu[e, 0 if kind == "g" else 1]
            put(i, rows, dot_tn(a, b))
            return c

        lax.fori_loop(0, 2, body, 0)

    def sa_copy(m, d):
        return pltpu.make_async_remote_copy(
            src_ref=sa.at[m % 2, pl.ds(256 * d, 256)],
            dst_ref=ra.at[m, d],
            send_sem=sa_s.at[m, d],
            recv_sem=ra_r.at[m, d],
            device_id=((right, left)[d], me),
            device_id_type=MESH,
        )

    def sb_copy(m, d):
        return pltpu.make_async_remote_copy(
            src_ref=sb.at[m % 2, d],
            dst_ref=rb.at[m, d],
            send_sem=sb_s.at[m, d],
            recv_sem=rb_r.at[m, d],
            device_id=((right, left)[d], me),
            device_id_type=MESH,
        )

    def step_a(m):
        if m >= 2:
            for d in range(2):
                sa_copy(m - 2, d).wait_send()

        def put(i, rows, value):
            sa[m % 2, rows, :] = value.astype(BF)

        partial(m, lax.rem(x + 2, NX), put)
        for d in range(2):
            sa_copy(m, d).start()

    def step_b(m):
        if m >= 2:
            for d in range(2):
                sb_copy(m - 2, d).wait_send()
        for d in range(2):
            sa_copy(m, d).wait_recv()

            def put(i, rows, value):
                add = jnp.where(i == d, ra[m, d].astype(F32), 0.0)
                sb[m % 2, d, rows, :] = (value + add).astype(BF)

            partial(m, (right, left)[d], put)
            sb_copy(m, d).start()

    outs = {"d": gd, "g": gg, "u": gu}

    def out_copy(m):
        kind, e = chunks[m]
        return pltpu.make_async_copy(outd if kind == "d" else outv.at[m % 2], outs[kind].at[e], out_sem.at[m])

    def own_part(m):
        def put(i, rows, value):
            own[rows, :] = value

        partial(m, x, put)

    def final(m):
        kind, e = chunks[m]
        own_part(m)
        if m == 1:
            out_copy(0).wait()
        if m >= 4:
            out_copy(m - 2).wait()
        for d in range(2):
            sb_copy(m, d).wait_recv()
            pltpu.make_async_copy(rb.at[m, d], rbv.at[d], ld_sem.at[d]).start()
        for d in range(2):
            pltpu.make_async_copy(rb.at[m, d], rbv.at[d], ld_sem.at[d]).wait()

        def body(i, c):
            rows = pl.ds(pl.multiple_of(i * 128, 128), 128)
            total = own[rows, :] + rbv[0, rows, :].astype(F32) + rbv[1, rows, :].astype(F32)
            if kind == "d":
                outd[:, rows] = total.T.astype(BF)
            else:
                outv[m % 2, rows, :] = total.astype(BF)
            return c

        lax.fori_loop(0, 4, body, 0)
        out_copy(m).start()

    def combine():
        rank = tab[:, 0:64]
        dvals = jnp.zeros((128, 64), F32)
        for half in range(2):
            wait_back(half)
            load = pltpu.make_async_copy(back.at[half], bkv, ld_sem.at[3])
            load.start()
            spread = jnp.where(iota((64, 512), 0) == 2 * (iota((64, 512), 1) // 16) + half, 1.0, 0.0).astype(BF)
            wide = dot(rank, spread)
            lane = iota((128, 512), 1) % 16
            pm = jnp.where(wide == (lane + 1).astype(F32), 1.0, 0.0).astype(BF)
            load.wait()
            for n in range(4):
                cols = slice(512 * n, 512 * n + 512)
                got = dot(pm, bkv[:, :, cols].reshape(512, 512))
                tokacc[:, cols] = got if half == 0 else tokacc[:, cols] + got
            over = bkv[:, :, D : D + 256].reshape(512, 256)
            info = bkv[:, :, D + 256 :].reshape(512, 128).astype(F32)
            own_expert = iota((512, 64), 1) == 2 * (iota((512, 64), 0) // 16) + half
            for q in range(8):
                po = jnp.where((wide == (17 + lane // 8).astype(F32)) & (lane % 8 == q), 1.0, 0.0).astype(BF)
                cols = slice(256 * q, 256 * q + 256)
                tokacc[:, cols] = tokacc[:, cols] + dot(po, over)
                if q == 0:
                    dvals = dvals + dot(po, jnp.where(own_expert, info[:, 1:2], 0.0).astype(BF))
            dvals = dvals + dot(pm, jnp.where(own_expert, info[:, 0:1], 0.0).astype(BF))
        gtok[...] = tokacc[...].astype(BF)
        expert = iota((128, 64), 1)
        picked = [
            jnp.sum(jnp.where(ids[:, k : k + 1] == expert, dvals, 0.0), axis=1, keepdims=True) for k in range(8)
        ]
        dgate = jnp.concatenate(picked, axis=1)
        pr = probs[...]
        glog[...] = pr * (dgate - jnp.sum(pr * dgate, axis=1, keepdims=True))

    forward(0)
    start_weights(1)
    dispatch(ug, us, False)
    step_a(0)
    forward(1)
    start_weights(0)
    step_a(1)
    step_b(0)
    backward(0)
    step_a(2)
    step_b(1)
    backward(1)
    final(0)
    step_a(3)
    step_b(2)
    input_grad(0)
    start_weights(1)
    send_back(0)
    input_grad(1)
    send_back(1)
    final(1)
    step_a(4)
    step_b(3)
    final(2)
    step_a(5)
    step_b(4)
    final(3)
    step_b(5)
    final(4)
    combine()
    final(5)
    for m in (4, 5):
        for d in range(2):
            sa_copy(m, d).wait_send()
            sb_copy(m, d).wait_send()
    for m in (1, 4, 5):
        out_copy(m).wait()


def on_device(tokens, expert_ids, gate_logits, upstream, w_gate, w_up, w_down):
    probs = jax.nn.softmax(gate_logits, axis=-1)
    tab = routing_table(expert_ids, probs.astype(BF).astype(F32))
    tg = lax.all_gather(jnp.concatenate([tokens, tab], axis=1), "expert").reshape(16, 256, D + 128)
    ug = lax.all_gather(upstream, "expert").reshape(16, 256, D)
    sd = jax.ShapeDtypeStruct
    dma = pltpu.SemaphoreType.DMA
    vm = pltpu.VMEM
    res = pl.pallas_call(
        kernel,
        out_shape=(
            sd((128, D), BF),
            sd((128, 8), F32),
            sd((2, 512, FF), BF),
            sd((2, 512, FF), BF),
            sd((2, FF, 512), BF),
            sd((6, 2, 512, FF), BF),
            sd((2, NE, 16, BACK), BF),
        ),
        in_specs=[ANY] * 5 + [VMEM] * 3,
        out_specs=(VMEM, VMEM, ANY, ANY, ANY, ANY, ANY),
        scratch_shapes=[
            vm((2, 256, D + 128), BF),
            vm((16, 80, 256), BF),
            vm((2, ROWS, D), BF),
            vm((2, ROWS, D), BF),
            vm((128, D + 128), F32),
            vm((2, ROWS, 128), F32),
            vm((D, FF), BF),
            vm((D, FF), BF),
            vm((FF, D), BF),
            vm((2, ROWS, FF), F32),
            vm((2, ROWS, FF), F32),
            vm((2, ROWS, FF), BF),
            vm((2, 2, ROWS, FF), BF),
            vm((2, ROWS, 128), F32),
            vm((2, 512, FF), BF),
            vm((6, 2, 256, FF), BF),
            vm((2, 2, 512, FF), BF),
            vm((2, 512, FF), BF),
            vm((512, FF), F32),
            vm((2, 512, FF), BF),
            vm((FF, 512), BF),
            vm((2, ROWS, BACK), BF),
            vm((NE, 16, BACK), BF),
            vm((128, D), F32),
            dma((2,)),
            dma((3,)),
            dma((6, 2)),
            dma((6, 2)),
            dma((6, 2)),
            dma((6, 2)),
            dma((2,)),
            dma((2,)),
            dma((4,)),
            dma((6,)),
        ],
        compiler_params=pltpu.CompilerParams(collective_id=0, has_side_effects=True, vmem_limit_bytes=64 << 20),
        cost_estimate=pl.CostEstimate(flops=29 * 10**9, bytes_accessed=10**8, transcendentals=10**6),
        name="expert_backward",
    )(tg, ug, w_gate, w_up, w_down, tab, expert_ids, probs)
    return res[:5]


def solution(mesh):
    rows = P(("dp", "expert"), None)
    whole = P("expert", None, None)
    return jax.shard_map(
        on_device,
        mesh=mesh,
        in_specs=(rows, rows, rows, rows, whole, whole, whole),
        out_specs=(rows, rows, P("expert", "dp", None), P("expert", "dp", None), P("expert", None, "dp")),
        check_vma=False,
    )
```

```python
import jax
import jax.numpy as jnp
from jax import lax
from jax.experimental import pallas as pl
from jax.experimental.pallas import tpu as pltpu
from jax.sharding import PartitionSpec as P

MESH = pl.DeviceIdType.MESH
BF = jnp.bfloat16
F32 = jnp.float32
D, FF, NE, NX = 2048, 768, 32, 4
MAIN, OVF = 16, 2
ROWS = NE * (MAIN + OVF)
BACK = D + 256 + 128
ANY = pl.BlockSpec(memory_space=pl.ANY)
VMEM = pl.BlockSpec(memory_space=pltpu.VMEM)


def iota(shape, dim):
    return lax.broadcasted_iota(jnp.int32, shape, dim)


def dot_nt(a, b):
    return lax.dot_general(a, b, (((1,), (1,)), ((), ())), preferred_element_type=F32)


def dot_tn(a, b):
    return lax.dot_general(a, b, (((0,), (0,)), ((), ())), preferred_element_type=F32)


def dot(a, b):
    return jnp.dot(a, b, preferred_element_type=F32)


def routing_table(ids, gate_rounded):
    expert = iota((128, 64), 1)
    routed = jnp.zeros((128, 64), F32)
    gates = jnp.zeros((128, 64), F32)
    for k in range(8):
        hit = ids[:, k : k + 1] == expert
        routed = routed + jnp.where(hit, 1.0, 0.0)
        gates = gates + jnp.where(hit, gate_rounded[:, k : k + 1], 0.0)
    before = jnp.where(iota((128, 128), 1) < iota((128, 128), 0), 1.0, 0.0)
    rank = dot(before.astype(BF), routed.astype(BF))
    return jnp.concatenate([jnp.where(routed > 0, rank + 1.0, 0.0), gates], axis=1).astype(BF)


def slot_targets():
    row, lane = iota((80, 256), 0), iota((80, 256), 1)
    over = row - 64
    core = jnp.where(row < 64, (row % 32) // 16, (over % 4) // 2)
    slot = jnp.where(row < 64, row % 16, 16 + over % 2)
    ok = (core == lane // 128) & (row < 72)
    second = ((row >= 32) & (row < 64)) | (over >= 4)
    return jnp.where(ok, slot + 1, -1).astype(F32), jnp.where(second, 1.0, 0.0)


JOBS = ((1152, 1024), (256, 256), (512, 512), (256, 256))


def kernel(
    tokens, upstream, wg, wu, wd, ids, logits,
    gtok, glog, gg, gu, gd, rb, back, g00, g01, g10, g11, g20, g21, g30, g31,
    tab, first, stage, pmat, xs, us, ov, xgate, wgv, wuv, wdv, pre_g, pre_u, wh, dgu, dgacc,
    sa, ra, sb, rbv, own, outv, outd, dxs, bkv, tokacc,
    ag_s, ag_r, ag_l, stage_sem, w_sem, sa_s, ra_r, sb_s, rb_r, bk_s, bk_r, ld_sem, out_sem,
):
    gathered = ((g00, g01), (g10, g11), (g20, g21), (g30, g31))
    x, me = lax.axis_index("dp"), lax.axis_index("expert")
    right, left = lax.rem(x + 1, NX), lax.rem(x + 3, NX)
    z, y, core = me // 8, (me // 2) % 4, me % 2

    barrier = pltpu.get_barrier_semaphore()

    def greet(i, c):
        pl.semaphore_signal(barrier, inc=1, device_id=(x, lax.rem(me + i, NE)), device_id_type=MESH)
        return c

    lax.fori_loop(1, NE, greet, 0)
    for other in (right, left):
        pl.semaphore_signal(barrier, inc=1, device_id=(other, me), device_id_type=MESH)

    def wload(e):
        return [
            pltpu.make_async_copy(wg.at[e], wgv, w_sem.at[0]),
            pltpu.make_async_copy(wu.at[e], wuv, w_sem.at[1]),
        ]

    def wdload(e):
        return pltpu.make_async_copy(wd.at[e], wdv, w_sem.at[2])

    def start_weights(e):
        for cp in wload(e):
            cp.start()

    start_weights(0)
    wdload(0).start()

    def place(r, a, b):
        return (b, a) if r == 0 else (a, b)

    def peer(r, a, b):
        pz, py = place(r, a % 4, b % 4)
        return (pz * 4 + py) * 2 + core

    pos = ((y, z), (z, y))

    def chunk(j, r, b, half=None):
        g = gathered[j][r]
        span = pl.ds(0, 4) if half is None else pl.ds(2 * half, 2)
        return g.at[b % 4, span, core] if r == 0 else g.at[span, b % 4, core]

    def block(j, r, a):
        pz, py = place(r, a % 4, pos[r][1])
        return gathered[j][r].at[pz, py, core]

    def source(j, r):
        if j == 0:
            return first if r == 0 else tokens.at[:, pl.ds(1024, 1024)]
        if j == 2:
            return upstream.at[:, pl.ds(pl.multiple_of(512 * (right, left)[r], 512), 512)]
        quarter = lax.rem(x + 2, NX) if j == 1 else x
        return upstream.at[:, pl.ds(pl.multiple_of(512 * quarter + 256 * r, 256), 256)]

    def ag(j, r, k):
        p1, p2 = pos[r]
        if k < 2:
            src, dst = source(j, r), block(j, r, p1)
        elif k < 4:
            rows = pl.ds(64 * (k - 2), 64)
            src = dst = block(j, r, p1 + (3, 1)[k - 2]).at[rows]
        elif k < 6:
            src = dst = chunk(j, r, p2)
        elif k < 8:
            src = dst = chunk(j, r, p2 + (3, 1)[k - 6], half=k - 6)
        else:
            src = dst = chunk(j, r, p2 + (0, 3, 1, 2)[k - 8])
        if k < 4:
            to = peer(r, p1 + (1, 3)[k % 2], p2)
        elif k < 8:
            to = peer(r, p1, p2 + (1, 3)[k % 2])
        else:
            to = (z * 4 + y) * 2 + 1 - core
        return pltpu.make_async_remote_copy(
            src_ref=src,
            dst_ref=dst,
            send_sem=ag_s.at[j, r, k],
            recv_sem=ag_r.at[j, r, k],
            device_id=(x, to),
            device_id_type=MESH,
        )

    def keep(j, r):
        return pltpu.make_async_copy(source(j, r), block(j, r, pos[r][0]), ag_l.at[j, r])

    def ag_own(j):
        for r in range(2):
            ag(j, r, 0).start()
            ag(j, r, 1).start()
            keep(j, r).start()

    def ag_ring(j):
        for r in range(2):
            for k in range(2):
                ag(j, r, k).wait_recv()
                ag(j, r, k + 2).start()

    def ag_chunk(j):
        for r in range(2):
            ag(j, r, 2).wait_recv()
            ag(j, r, 3).wait_recv()
            keep(j, r).wait()
            for k in (4, 5, 8):
                ag(j, r, k).start()

    def ag_forward(j):
        for r in range(2):
            for k in range(2):
                ag(j, r, k + 4).wait_recv()
                ag(j, r, k + 6).start()
                ag(j, r, k + 9).start()

    def ag_last(j):
        for r in range(2):
            ag(j, r, 6).wait_recv()
            ag(j, r, 7).wait_recv()
            ag(j, r, 11).start()

    target, second = slot_targets()

    def load(j, r, b, slot):
        g = gathered[j][r]
        src = g.at[b] if r == 0 else g.at[:, b]
        return pltpu.make_async_copy(src, stage.at[slot, :, :, :, pl.ds(0, JOBS[j][r])], stage_sem.at[slot])

    def column(j, r):
        if j == 0:
            return 1024 * r
        if j == 2:
            return pl.multiple_of(512 * (right, left)[r], 512)
        return pl.multiple_of(512 * (lax.rem(x + 2, NX) if j == 1 else x) + 256 * r, 256)

    def pieces(j, r):
        w = JOBS[j][r]
        return [(at, min(512, w - at)) for at in range(0, w, 512)]

    def multiply(j, r, b, slot):
        dst = xs if j == 0 else us
        base = column(j, r)

        def body(k, c):
            pz, py = place(r, k, b)
            chip = pz * 4 + py
            at = pl.multiple_of(32 * chip, 32)
            at8 = pl.multiple_of(8 * chip, 8)
            if j == 0 and r == 0:
                tabj = stage[slot, k, :, :, 1024:1152].reshape(256, 128)
                pick = jnp.where(iota((8, 128), 1) == 2 * me + iota((8, 128), 0), 1.0, 0.0).astype(BF)
                ranks = dot_nt(pick, tabj)
                row0 = jnp.broadcast_to(ranks[0:1, :], (80, 256))
                row1 = jnp.broadcast_to(ranks[1:2, :], (80, 256))
                pm = jnp.where(jnp.where(second > 0.5, row1, row0) == target, 1.0, 0.0).astype(BF)
                pmat[chip] = pm
                got = dot(pm, tabj)
                xgate[0, pl.ds(at, 32), :] = got[0:32]
                xgate[1, pl.ds(at, 32), :] = got[32:64]
                ov[pl.ds(at8, 8), D : D + 128] = got[64:72]
            pm = pmat[chip]
            for off, w in pieces(j, r):
                if w == 128:
                    continue
                got = dot(pm, stage[slot, k, :, :, off : off + w].reshape(256, w))
                cols = pl.ds(base + off, w)
                dst[0, pl.ds(at, 32), cols] = got[0:32].astype(BF)
                dst[1, pl.ds(at, 32), cols] = got[32:64].astype(BF)
                ov[pl.ds(at8, 8), cols] = got[64:72]
            return c

        lax.fori_loop(0, 4, body, 0)

    def overflow(j, r):
        dst = xs if j == 0 else us
        row, col = iota((64, 128), 0), iota((64, 128), 1)
        for e in range(2):
            sel = jnp.where(col == 8 * (row // 4) + 4 * e + row % 4, 1.0, 0.0).astype(BF)
            for off, w in pieces(j, r):
                if w == 128:
                    xgate[e, 512:576, :] = dot(sel, ov[:, D : D + 128].astype(BF))
                    continue
                cols = pl.ds(column(j, r) + off, w)
                dst[e, 512:576, cols] = dot(sel, ov[:, cols].astype(BF)).astype(BF)

    def dispatch_one(j, r, n):
        b = (pos[r][1] + (0, 3, 1, 2)[n]) % 4
        ag(j, r, 8 + n).wait_recv()
        load(j, r, b, 0).start()
        load(j, r, b, 0).wait()
        multiply(j, r, b, 0)

    def dispatch(j, r):
        for n in range(4):
            ag(j, r, 8 + n).wait_recv()
        load(j, r, 0, 0).start()

        def body(b, c):
            slot = lax.rem(b, 2)

            @pl.when(b < 3)
            def _():
                load(j, r, b + 1, 1 - slot).start()

            load(j, r, b, slot).wait()
            multiply(j, r, b, slot)
            return c

        lax.fori_loop(0, 4, body, 0)
        overflow(j, r)

    def gate_of(e, rows):
        lane = iota((rows.size, 128), 1)
        return jnp.sum(jnp.where(lane == 64 + 2 * me + e, xgate[e, rows, :], 0.0), axis=1, keepdims=True)

    def forward(e):
        for cp in wload(e):
            cp.wait()

        def body(i, c):
            rows = pl.ds(pl.multiple_of((i // 3) * 192, 192), 192)
            cols = pl.ds(pl.multiple_of((i % 3) * 256, 256), 256)
            pg = dot(xs[e, rows, :], wgv[:, cols])
            pu = dot(xs[e, rows, :], wuv[:, cols])
            pre_g[e, rows, cols] = pg
            pre_u[e, rows, cols] = pu
            hidden = pg * jax.nn.sigmoid(pg) * pu
            wh[e, rows, cols] = (gate_of(e, rows) * hidden).astype(BF)
            return c

        lax.fori_loop(0, 9, body, 0)

    def backward(e):
        wdload(e).wait()

        def body(i, c):
            rows = pl.ds(pl.multiple_of((i // 3) * 192, 192), 192)
            cols = pl.ds(pl.multiple_of((i % 3) * 256, 256), 256)
            raw = dot_nt(us[e, rows, :], wdv[cols, :])
            pg, pu = pre_g[e, rows, cols], pre_u[e, rows, cols]
            s = jax.nn.sigmoid(pg)
            act = pg * s
            part = raw * (act * pu)
            part = part[:, 0:128] + part[:, 128:256]
            dgacc[e, rows, :] = jnp.where(i % 3 == 0, jnp.zeros_like(part), dgacc[e, rows, :]) + part
            dh = gate_of(e, rows) * raw
            dgu[e, 0, rows, cols] = (dh * pu * s * (1.0 + pg * (1.0 - s))).astype(BF)
            dgu[e, 1, rows, cols] = (dh * act).astype(BF)
            return c

        lax.fori_loop(0, 9, body, 0)
        if e == 0:
            wdload(1).start()

    def input_grad(e):
        for cp in wload(e):
            cp.wait()

        def body(i, c):
            rows = pl.ds(pl.multiple_of((i // 4) * 192, 192), 192)
            cols = pl.ds(pl.multiple_of((i % 4) * 512, 512), 512)
            dx = dot_nt(dgu[e, 0, rows, :], wgv[cols, :]) + dot_nt(dgu[e, 1, rows, :], wuv[cols, :])
            dxs[e, rows, cols] = dx.astype(BF)
            return c

        lax.fori_loop(0, 12, body, 0)
        r, col = iota((512, 64), 0), iota((512, 64), 1)
        place = 2 * (r // 16) + (r % 16) // 8 == col
        packed = jnp.zeros((512, 256), F32)
        for q in range(8):
            sel = jnp.where(place & (r % 8 == q), 1.0, 0.0).astype(BF)
            packed = packed + dot(sel, dxs[e, 512:576, 256 * q : 256 * q + 256])
        dxs[e, 0:512, D : D + 256] = packed.astype(BF)
        dgate = jnp.sum(dgacc[e], axis=1, keepdims=True).astype(BF).astype(F32)
        first = iota((512, 128), 1) == 0
        sel = jnp.where(place & (r % 8 == 0), 1.0, 0.0).astype(BF)
        over = dot(sel, jnp.broadcast_to(dgate[512:576], (64, 128)).astype(BF))
        main = jnp.broadcast_to(dgate[0:512], (512, 128))
        dxs[e, 0:512, D + 256 :] = jnp.where(first, main, over).astype(BF)

    def send_back(e):
        pltpu.make_async_copy(dxs.at[e, pl.ds(pl.multiple_of(16 * me, 16), 16)], back.at[e, me], ld_sem.at[2]).start()

        def body(i, c):
            p = lax.rem(me + i, NE)
            pltpu.make_async_remote_copy(
                src_ref=dxs.at[e, pl.ds(pl.multiple_of(16 * p, 16), 16)],
                dst_ref=back.at[e, me],
                send_sem=bk_s.at[e],
                recv_sem=bk_r.at[e],
                device_id=(x, p),
                device_id_type=MESH,
            ).start()
            return c

        lax.fori_loop(1, NE, body, 0)
        pltpu.make_async_copy(dxs.at[e, pl.ds(pl.multiple_of(16 * me, 16), 16)], back.at[e, me], ld_sem.at[2]).wait()

    def wait_back(e):
        part = back.at[e, pl.ds(0, NE - 1)]
        pltpu.make_async_copy(part, part, bk_s.at[e]).wait()
        pltpu.make_async_copy(part, part, bk_r.at[e]).wait()

    chunks = [("d", 0), ("d", 1), ("g", 0), ("u", 0), ("g", 1), ("u", 1)]

    def partial(m, quarter, put):
        kind, e = chunks[m]

        def body(i, c):
            rows = pl.ds(pl.multiple_of(i * 256, 256), 256)
            cols = pl.ds(pl.multiple_of(quarter * 512 + i * 256, 256), 256)
            a = (us if kind == "d" else xs)[e, :, cols]
            b = wh[e] if kind == "d" else dgu[e, 0 if kind == "g" else 1]
            put(i, rows, dot_tn(a, b))
            return c

        lax.fori_loop(0, 2, body, 0)

    def sa_copy(m, d):
        return pltpu.make_async_remote_copy(
            src_ref=sa.at[m % 2, pl.ds(256 * d, 256)],
            dst_ref=ra.at[m, d],
            send_sem=sa_s.at[m, d],
            recv_sem=ra_r.at[m, d],
            device_id=((right, left)[d], me),
            device_id_type=MESH,
        )

    def sb_copy(m, d):
        return pltpu.make_async_remote_copy(
            src_ref=sb.at[m % 2, d],
            dst_ref=rb.at[m, d],
            send_sem=sb_s.at[m, d],
            recv_sem=rb_r.at[m, d],
            device_id=((right, left)[d], me),
            device_id_type=MESH,
        )

    def step_a(m):
        if m >= 2:
            for d in range(2):
                sa_copy(m - 2, d).wait_send()

        def put(i, rows, value):
            sa[m % 2, rows, :] = value.astype(BF)

        partial(m, lax.rem(x + 2, NX), put)
        for d in range(2):
            sa_copy(m, d).start()

    def step_b(m):
        if m >= 2:
            for d in range(2):
                sb_copy(m - 2, d).wait_send()
        for d in range(2):
            sa_copy(m, d).wait_recv()

            def put(i, rows, value):
                add = jnp.where(i == d, ra[m, d].astype(F32), 0.0)
                sb[m % 2, d, rows, :] = (value + add).astype(BF)

            partial(m, (right, left)[d], put)
            sb_copy(m, d).start()

    outs = {"d": gd, "g": gg, "u": gu}

    def out_copy(m):
        kind, e = chunks[m]
        return pltpu.make_async_copy(outd if kind == "d" else outv.at[m % 2], outs[kind].at[e], out_sem.at[m])

    def own_part(m):
        def put(i, rows, value):
            own[rows, :] = value

        partial(m, x, put)

    def final(m):
        kind, e = chunks[m]
        own_part(m)
        if m == 1:
            out_copy(0).wait()
        if m >= 4:
            out_copy(m - 2).wait()
        for d in range(2):
            sb_copy(m, d).wait_recv()
            pltpu.make_async_copy(rb.at[m, d], rbv.at[d], ld_sem.at[d]).start()
        for d in range(2):
            pltpu.make_async_copy(rb.at[m, d], rbv.at[d], ld_sem.at[d]).wait()

        def body(i, c):
            rows = pl.ds(pl.multiple_of(i * 128, 128), 128)
            total = own[rows, :] + rbv[0, rows, :].astype(F32) + rbv[1, rows, :].astype(F32)
            if kind == "d":
                outd[:, rows] = total.T.astype(BF)
            else:
                outv[m % 2, rows, :] = total.astype(BF)
            return c

        lax.fori_loop(0, 4, body, 0)
        out_copy(m).start()

    def combine():
        rank = tab[:, 0:64]
        dvals = jnp.zeros((128, 64), F32)
        for half in range(2):
            wait_back(half)
            load = pltpu.make_async_copy(back.at[half], bkv, ld_sem.at[3])
            load.start()
            spread = jnp.where(iota((64, 512), 0) == 2 * (iota((64, 512), 1) // 16) + half, 1.0, 0.0).astype(BF)
            wide = dot(rank, spread)
            lane = iota((128, 512), 1) % 16
            pm = jnp.where(wide == (lane + 1).astype(F32), 1.0, 0.0).astype(BF)
            load.wait()
            for n in range(4):
                cols = slice(512 * n, 512 * n + 512)
                got = dot(pm, bkv[:, :, cols].reshape(512, 512))
                tokacc[:, cols] = got if half == 0 else tokacc[:, cols] + got
            over = bkv[:, :, D : D + 256].reshape(512, 256)
            info = bkv[:, :, D + 256 :].reshape(512, 128).astype(F32)
            own_expert = iota((512, 64), 1) == 2 * (iota((512, 64), 0) // 16) + half
            for q in range(8):
                po = jnp.where((wide == (17 + lane // 8).astype(F32)) & (lane % 8 == q), 1.0, 0.0).astype(BF)
                cols = slice(256 * q, 256 * q + 256)
                tokacc[:, cols] = tokacc[:, cols] + dot(po, over)
                if q == 0:
                    dvals = dvals + dot(po, jnp.where(own_expert, info[:, 1:2], 0.0).astype(BF))
            dvals = dvals + dot(pm, jnp.where(own_expert, info[:, 0:1], 0.0).astype(BF))
        gtok[...] = tokacc[...].astype(BF)
        expert = iota((128, 64), 1)
        picked = [
            jnp.sum(jnp.where(ids[:, k : k + 1] == expert, dvals, 0.0), axis=1, keepdims=True) for k in range(8)
        ]
        dgate = jnp.concatenate(picked, axis=1)
        glog[...] = probs * (dgate - jnp.sum(probs * dgate, axis=1, keepdims=True))

    left_half = pltpu.make_async_copy(tokens.at[:, pl.ds(0, 1024)], first.at[:, pl.ds(0, 1024)], ld_sem.at[3])
    left_half.start()
    raised = jnp.exp(logits[...] - jnp.max(logits[...], axis=1, keepdims=True))
    probs = raised / jnp.sum(raised, axis=1, keepdims=True)
    tab[...] = routing_table(ids[...], probs.astype(BF).astype(F32))
    first[:, 1024:1152] = tab[...]
    left_half.wait()
    pl.semaphore_wait(barrier, NE - 1 + 2)

    ag_own(0)
    ag_ring(0)
    ag_chunk(0)
    ag_own(1)
    dispatch_one(0, 0, 0)
    ag_ring(1)
    ag_forward(0)
    ag_chunk(1)
    dispatch_one(0, 0, 1)
    dispatch_one(0, 0, 2)
    ag_last(0)
    ag_own(2)
    ag_forward(1)
    dispatch_one(0, 0, 3)
    overflow(0, 0)
    dispatch(0, 1)
    ag_ring(2)
    ag_chunk(2)
    forward(0)
    start_weights(1)
    ag_last(1)
    dispatch(1, 0)
    dispatch(1, 1)
    step_a(0)
    ag_own(3)
    ag_ring(3)
    ag_forward(2)
    forward(1)
    start_weights(0)
    step_a(1)
    ag_chunk(3)
    ag_last(2)
    dispatch(2, 0)
    dispatch(2, 1)
    step_b(0)
    ag_forward(3)
    step_b(1)
    ag_last(3)
    dispatch(3, 0)
    dispatch(3, 1)
    backward(0)
    step_a(2)
    backward(1)
    final(0)
    step_a(3)
    step_b(2)
    input_grad(0)
    start_weights(1)
    send_back(0)
    input_grad(1)
    send_back(1)
    final(1)
    step_a(4)
    step_b(3)
    final(2)
    step_a(5)
    step_b(4)
    final(3)
    step_b(5)
    final(4)
    combine()
    final(5)
    for m in (4, 5):
        for d in range(2):
            sa_copy(m, d).wait_send()
            sb_copy(m, d).wait_send()
    for m in (1, 4, 5):
        out_copy(m).wait()
    for j in range(4):
        for r in range(2):
            for k in range(12):
                ag(j, r, k).wait_send()


def on_device(tokens, expert_ids, gate_logits, upstream, w_gate, w_up, w_down):
    sd = jax.ShapeDtypeStruct
    dma = pltpu.SemaphoreType.DMA
    vm = pltpu.VMEM
    res = pl.pallas_call(
        kernel,
        out_shape=(
            sd((128, D), BF),
            sd((128, 8), F32),
            sd((2, 512, FF), BF),
            sd((2, 512, FF), BF),
            sd((2, FF, 512), BF),
            sd((6, 2, 512, FF), BF),
            sd((2, NE, 16, BACK), BF),
            *[sd((4, 4, 2, 128, w), BF) for pair in JOBS for w in pair],
        ),
        in_specs=[ANY] * 5 + [VMEM] * 2,
        out_specs=(VMEM, VMEM) + (ANY,) * 13,
        scratch_shapes=[
            vm((128, 128), BF),
            vm((128, 1152), BF),
            vm((2, 4, 2, 128, 1152), BF),
            vm((16, 80, 256), BF),
            vm((2, ROWS, D), BF),
            vm((2, ROWS, D), BF),
            vm((128, D + 128), F32),
            vm((2, ROWS, 128), F32),
            vm((D, FF), BF),
            vm((D, FF), BF),
            vm((FF, D), BF),
            vm((2, ROWS, FF), F32),
            vm((2, ROWS, FF), F32),
            vm((2, ROWS, FF), BF),
            vm((2, 2, ROWS, FF), BF),
            vm((2, ROWS, 128), F32),
            vm((2, 512, FF), BF),
            vm((6, 2, 256, FF), BF),
            vm((2, 2, 512, FF), BF),
            vm((2, 512, FF), BF),
            vm((512, FF), F32),
            vm((2, 512, FF), BF),
            vm((FF, 512), BF),
            vm((2, ROWS, BACK), BF),
            vm((NE, 16, BACK), BF),
            vm((128, D), F32),
            dma((4, 2, 12)),
            dma((4, 2, 12)),
            dma((4, 2)),
            dma((2,)),
            dma((3,)),
            dma((6, 2)),
            dma((6, 2)),
            dma((6, 2)),
            dma((6, 2)),
            dma((2,)),
            dma((2,)),
            dma((4,)),
            dma((6,)),
        ],
        compiler_params=pltpu.CompilerParams(collective_id=0, has_side_effects=True, vmem_limit_bytes=64 << 20),
        cost_estimate=pl.CostEstimate(flops=29 * 10**9, bytes_accessed=10**8, transcendentals=10**6),
        name="expert_backward",
    )(tokens, upstream, w_gate, w_up, w_down, expert_ids, gate_logits)
    return res[:5]


def solution(mesh):
    rows = P(("dp", "expert"), None)
    whole = P("expert", None, None)
    return jax.shard_map(
        on_device,
        mesh=mesh,
        in_specs=(rows, rows, rows, rows, whole, whole, whole),
        out_specs=(rows, rows, P("expert", "dp", None), P("expert", "dp", None), P("expert", None, "dp")),
        check_vma=False,
    )
```

```python
import jax
import jax.numpy as jnp
from jax import lax
from jax.experimental import pallas as pl
from jax.experimental.pallas import tpu as pltpu
from jax.sharding import PartitionSpec as P

MESH = pl.DeviceIdType.MESH
BF = jnp.bfloat16
F32 = jnp.float32
D, FF, NE, NX = 2048, 768, 32, 4
MAIN, OVF = 16, 2
ROWS = NE * (MAIN + OVF)
BACK = D + 256 + 128
ANY = pl.BlockSpec(memory_space=pl.ANY)
VMEM = pl.BlockSpec(memory_space=pltpu.VMEM)


def iota(shape, dim):
    return lax.broadcasted_iota(jnp.int32, shape, dim)


def dot_nt(a, b):
    return lax.dot_general(a, b, (((1,), (1,)), ((), ())), preferred_element_type=F32)


def dot_tn(a, b):
    return lax.dot_general(a, b, (((0,), (0,)), ((), ())), preferred_element_type=F32)


def dot(a, b):
    return jnp.dot(a, b, preferred_element_type=F32)


def slot_numbers(ids):
    expert = iota((128, 64), 1)
    routed = jnp.zeros((128, 64), F32)
    for k in range(8):
        routed = routed + jnp.where(ids[:, k : k + 1] == expert, 1.0, 0.0)
    before = jnp.where(iota((128, 128), 1) < iota((128, 128), 0), 1.0, 0.0)
    rank = dot(before.astype(BF), routed.astype(BF))
    return jnp.where(routed > 0, rank + 1.0, 0.0).astype(BF)


def slot_targets():
    row, lane = iota((80, 256), 0), iota((80, 256), 1)
    over = row - 64
    core = jnp.where(row < 64, (row % 32) // 16, (over % 4) // 2)
    slot = jnp.where(row < 64, row % 16, 16 + over % 2)
    ok = (core == lane // 128) & (row < 72)
    second = ((row >= 32) & (row < 64)) | (over >= 4)
    return jnp.where(ok, slot + 1, -1).astype(F32), jnp.where(second, 1.0, 0.0)


JOBS = (1024, 256, 256, 256, 256)
NJ = len(JOBS)


def kernel(
    tokens, upstream, wg, wu, wd, ids, logits,
    gtok, glog, gg, gu, gd, rb, back, g00, g01, g10, g11, g20, g21, g30, g31, g40, g41,
    meta, metas, ranks, stage, pmat, xs, us, ov, xgate, wgv, wuv, wdv, pre_g, pre_u, wh, dgu, dgacc,
    sa, ra, sb, rbv, own, outv, outd, dxs, tokacc,
    mt_s, mt_r, ag_s, ag_r, ag_l, stage_sem, w_sem, sa_s, ra_r, sb_s, rb_r, bk_s, bk_r, bk_l, ld_sem, out_sem,
):
    gathered = ((g00, g01), (g10, g11), (g20, g21), (g30, g31), (g40, g41))
    x, me = lax.axis_index("dp"), lax.axis_index("expert")
    right, left = lax.rem(x + 1, NX), lax.rem(x + 3, NX)
    z, y, core = me // 8, (me // 2) % 4, me % 2

    barrier = pltpu.get_barrier_semaphore()

    def greet(i, c):
        pl.semaphore_signal(barrier, inc=1, device_id=(x, lax.rem(me + i, NE)), device_id_type=MESH)
        return c

    lax.fori_loop(1, NE, greet, 0)
    for other in (right, left):
        pl.semaphore_signal(barrier, inc=1, device_id=(other, me), device_id_type=MESH)

    def wload(e):
        return [
            pltpu.make_async_copy(wg.at[e], wgv, w_sem.at[0]),
            pltpu.make_async_copy(wu.at[e], wuv, w_sem.at[1]),
        ]

    def wdload(e):
        return pltpu.make_async_copy(wd.at[e], wdv, w_sem.at[2])

    def start_weights(e):
        for cp in wload(e):
            cp.start()

    def place(r, a, b):
        return (b, a) if r == 0 else (a, b)

    def peer(r, a, b):
        pz, py = place(r, a % 4, b % 4)
        return (pz * 4 + py) * 2 + core

    pos = ((y, z), (z, y))

    def chunk(j, r, b, half=None):
        g = gathered[j][r]
        span = pl.ds(0, 4) if half is None else pl.ds(2 * half, 2)
        return g.at[b % 4, span, core] if r == 0 else g.at[span, b % 4, core]

    def block(j, r, a):
        pz, py = place(r, a % 4, pos[r][1])
        return gathered[j][r].at[pz, py, core]

    def column(j, r):
        if j == 0:
            return 1024 * r
        quarter = (lax.rem(x + 2, NX), (right, left)[r], (right, left)[r], x)[j - 1]
        return pl.multiple_of(512 * quarter + (256 * r, 0, 256, 256 * r)[j - 1], 256)

    def source(j, r):
        return dxs.at[min(j, 1), pl.ds(0, 128), pl.ds(column(j, r), JOBS[j])]

    def ag(j, r, k):
        p1, p2 = pos[r]
        if k < 2:
            src, dst = source(j, r), block(j, r, p1)
        elif k < 4:
            rows = pl.ds(64 * (k - 2), 64)
            src = dst = block(j, r, p1 + (3, 1)[k - 2]).at[rows]
        elif k < 6:
            src = dst = chunk(j, r, p2)
        elif k < 8:
            src = dst = chunk(j, r, p2 + (3, 1)[k - 6], half=k - 6)
        else:
            src = dst = chunk(j, r, p2 + (0, 3, 1, 2)[k - 8])
        if k < 4:
            to = peer(r, p1 + (1, 3)[k % 2], p2)
        elif k < 8:
            to = peer(r, p1, p2 + (1, 3)[k % 2])
        else:
            to = (z * 4 + y) * 2 + 1 - core
        return pltpu.make_async_remote_copy(
            src_ref=src,
            dst_ref=dst,
            send_sem=ag_s.at[j, r, k],
            recv_sem=ag_r.at[j, r, k],
            device_id=(x, to),
            device_id_type=MESH,
        )

    def keep(j, r):
        return pltpu.make_async_copy(source(j, r), block(j, r, pos[r][0]), ag_l.at[j, r])

    def ag_own(j):
        for r in range(2):
            ag(j, r, 0).start()
            ag(j, r, 1).start()
            keep(j, r).start()

    def ag_ring(j):
        for r in range(2):
            for k in range(2):
                ag(j, r, k).wait_recv()
                ag(j, r, k + 2).start()

    def ag_chunk(j):
        for r in range(2):
            ag(j, r, 2).wait_recv()
            ag(j, r, 3).wait_recv()
            keep(j, r).wait()
            for k in (4, 5, 8):
                ag(j, r, k).start()

    def ag_forward(j):
        for r in range(2):
            for k in range(2):
                ag(j, r, k + 4).wait_recv()
                ag(j, r, k + 6).start()
                ag(j, r, k + 9).start()

    def ag_last(j):
        for r in range(2):
            ag(j, r, 6).wait_recv()
            ag(j, r, 7).wait_recv()
            ag(j, r, 11).start()

    target, second = slot_targets()

    def order(r, n):
        return (pos[r][1] + (0, 3, 1, 2)[n]) % 4

    def load(j, r, n):
        g = gathered[j][r]
        b = order(r, n)
        part = (n % 2, 0, 1024) if j == 0 else ((j - 1) % 2, 256 * n, 256)
        src = g.at[b] if r == 0 else g.at[:, b]
        return pltpu.make_async_copy(
            src, stage.at[part[0], r, :, :, :, pl.ds(part[1], part[2])], stage_sem.at[part[0], r, 0 if j == 0 else n]
        )

    def fetch(j, n):
        for r in range(2):
            ag(j, r, 8 + n).wait_recv()
            load(j, r, n).start()

    def multiply(j, r, b, k, half, strip):
        dst = xs if j == 0 else us
        base = column(j, r)
        pz, py = place(r, k, b)
        chip = pz * 4 + py
        at = pl.multiple_of(32 * chip, 32)
        w = 512 if j == 0 else 256
        pm = pmat[chip]
        for off in range(0, JOBS[j], w):
            got = dot(pm, stage[half, r, k, :, :, pl.ds(strip + off, w)].reshape(256, w))
            cols = pl.ds(base + off, w)
            dst[0, pl.ds(at, 32), cols] = got[0:32].astype(BF)
            dst[1, pl.ds(at, 32), cols] = got[32:64].astype(BF)
            ov[pl.ds(pl.multiple_of(8 * chip, 8), 8), cols] = got[64:72]

    def dispatch_tokens(n):
        for r in range(2):
            load(0, r, n).wait()

            def body(k, c, r=r):
                multiply(0, r, order(r, n), k, n % 2, 0)
                return c

            lax.fori_loop(0, 4, body, 0)
        if n == 3:
            overflow(0, 0)
            overflow(0, 1)

    def dispatch_upstream(j):
        for r in range(2):
            for n in range(4):
                load(j, r, n).wait()

                def body(k, c, r=r, n=n):
                    multiply(j, r, order(r, n), k, (j - 1) % 2, 256 * n)
                    return c

                lax.fori_loop(0, 4, body, 0)
            overflow(j, r)

    def overflow(j, r):
        dst = xs if j == 0 else us
        row, col = iota((64, 128), 0), iota((64, 128), 1)
        w = 512 if j == 0 else 256
        for e in range(2):
            sel = jnp.where(col == 8 * (row // 4) + 4 * e + row % 4, 1.0, 0.0).astype(BF)
            for off in range(0, JOBS[j], w):
                cols = pl.ds(column(j, r) + off, w)
                dst[e, 512:576, cols] = dot(sel, ov[:, cols].astype(BF)).astype(BF)

    def share_routing():
        def body(i, c):
            p = lax.rem(me + i, NE)
            pltpu.make_async_remote_copy(
                src_ref=meta,
                dst_ref=metas.at[me],
                send_sem=mt_s,
                recv_sem=mt_r,
                device_id=(x, p),
                device_id_type=MESH,
            ).start()
            return c

        lax.fori_loop(1, NE, body, 0)

    def read_routing():
        metas[me] = meta[...]
        part = metas.at[pl.ds(0, NE - 1)]
        pltpu.make_async_copy(part, part, mt_s).wait()
        pltpu.make_async_copy(part, part, mt_r).wait()
        known = metas[...].astype(F32)
        before = jnp.where(iota((128, 128), 0) < iota((128, 128), 1), 1.0, 0.0).astype(BF)
        for e in range(2):
            hit = jnp.where(known[:, 0:8, :] == (2 * me + e).astype(F32), 1.0, 0.0)
            routed = jnp.sum(hit, axis=1)
            gates = jnp.sum(hit * known[:, 8:16, :], axis=1)
            number = jnp.where(routed > 0, dot(routed.astype(BF), before) + 1.0, 0.0)
            for h in range(2):
                pick = jnp.where(iota((16, NE), 1) == 2 * iota((16, NE), 0) + h, 1.0, 0.0).astype(BF)
                ranks[e, :, 128 * h : 128 * h + 128] = dot(pick, number.astype(BF))
                ranks[2 + e, :, 128 * h : 128 * h + 128] = dot(pick, gates.astype(BF))

    def build_dispatch():
        def body(chip, c):
            at = pl.multiple_of(32 * chip, 32)

            def rows(n):
                pair = [jnp.broadcast_to(ranks[n + e, pl.ds(chip, 1), :], (80, 256)) for e in range(2)]
                return jnp.where(second > 0.5, pair[1], pair[0])

            pm = jnp.where(rows(0) == target, 1.0, 0.0)
            pmat[chip] = pm.astype(BF)
            got = jnp.broadcast_to(jnp.sum(pm * rows(2), axis=1, keepdims=True), (80, 128))
            xgate[0, pl.ds(at, 32), :] = got[0:32]
            xgate[1, pl.ds(at, 32), :] = got[32:64]
            ov[pl.ds(pl.multiple_of(8 * chip, 8), 8), D : D + 128] = got[64:72]
            return c

        lax.fori_loop(0, 16, body, 0)
        row, col = iota((64, 128), 0), iota((64, 128), 1)
        for e in range(2):
            sel = jnp.where(col == 8 * (row // 4) + 4 * e + row % 4, 1.0, 0.0).astype(BF)
            xgate[e, 512:576, :] = dot(sel, ov[:, D : D + 128].astype(BF))

    def gate_of(e, rows):
        return xgate[e, rows, 0:1]

    def forward(e, lo, hi):
        if lo == 0:
            for cp in wload(e):
                cp.wait()

        def body(i, c):
            rows = pl.ds(pl.multiple_of((i // 3) * 192, 192), 192)
            cols = pl.ds(pl.multiple_of((i % 3) * 256, 256), 256)
            pg = dot(xs[e, rows, :], wgv[:, cols])
            pu = dot(xs[e, rows, :], wuv[:, cols])
            pre_g[e, rows, cols] = pg
            pre_u[e, rows, cols] = pu
            hidden = pg * jax.nn.sigmoid(pg) * pu
            wh[e, rows, cols] = (gate_of(e, rows) * hidden).astype(BF)
            return c

        lax.fori_loop(lo, hi, body, 0)

    def backward(e):
        wdload(e).wait()

        def body(i, c):
            rows = pl.ds(pl.multiple_of((i // 3) * 192, 192), 192)
            cols = pl.ds(pl.multiple_of((i % 3) * 256, 256), 256)
            raw = dot_nt(us[e, rows, :], wdv[cols, :])
            pg, pu = pre_g[e, rows, cols], pre_u[e, rows, cols]
            s = jax.nn.sigmoid(pg)
            act = pg * s
            part = raw * (act * pu)
            part = part[:, 0:128] + part[:, 128:256]
            dgacc[rows, :] = jnp.where(i % 3 == 0, jnp.zeros_like(part), dgacc[rows, :]) + part
            dh = gate_of(e, rows) * raw
            dgu[e, 0, rows, cols] = (dh * pu * s * (1.0 + pg * (1.0 - s))).astype(BF)
            dgu[e, 1, rows, cols] = (dh * act).astype(BF)
            return c

        lax.fori_loop(0, 9, body, 0)
        if e == 0:
            wdload(1).start()

    def input_grad(e):
        for cp in wload(e):
            cp.wait()

        def body(i, c):
            rows = pl.ds(pl.multiple_of((i // 4) * 192, 192), 192)
            cols = pl.ds(pl.multiple_of((i % 4) * 512, 512), 512)
            dx = dot_nt(dgu[e, 0, rows, :], wgv[cols, :]) + dot_nt(dgu[e, 1, rows, :], wuv[cols, :])
            dxs[e, rows, cols] = dx.astype(BF)
            return c

        lax.fori_loop(0, 12, body, 0)
        r, col = iota((512, 64), 0), iota((512, 64), 1)
        place = 2 * (r // 16) + (r % 16) // 8 == col
        packed = jnp.zeros((512, 256), F32)
        for q in range(8):
            sel = jnp.where(place & (r % 8 == q), 1.0, 0.0).astype(BF)
            packed = packed + dot(sel, dxs[e, 512:576, 256 * q : 256 * q + 256])
        dxs[e, 0:512, D : D + 256] = packed.astype(BF)
        dgate = jnp.sum(dgacc[...], axis=1, keepdims=True).astype(BF).astype(F32)
        first = iota((512, 128), 1) == 0
        sel = jnp.where(place & (r % 8 == 0), 1.0, 0.0).astype(BF)
        over = dot(sel, jnp.broadcast_to(dgate[512:576], (64, 128)).astype(BF))
        main = jnp.broadcast_to(dgate[0:512], (512, 128))
        dxs[e, 0:512, D + 256 :] = jnp.where(first, main, over).astype(BF)

    def send_back(e):
        pltpu.make_async_copy(dxs.at[e, pl.ds(pl.multiple_of(16 * me, 16), 16)], back.at[e, pl.ds(pl.multiple_of(16 * me, 16), 16)], ld_sem.at[2]).start()

        def body(i, c):
            p = lax.rem(me + i, NE)
            pltpu.make_async_remote_copy(
                src_ref=dxs.at[e, pl.ds(pl.multiple_of(16 * p, 16), 16)],
                dst_ref=back.at[e, pl.ds(pl.multiple_of(16 * me, 16), 16)],
                send_sem=bk_s.at[e],
                recv_sem=bk_r.at[e],
                device_id=(x, p),
                device_id_type=MESH,
            ).start()
            return c

        lax.fori_loop(1, NE, body, 0)
        pltpu.make_async_copy(dxs.at[e, pl.ds(pl.multiple_of(16 * me, 16), 16)], back.at[e, pl.ds(pl.multiple_of(16 * me, 16), 16)], ld_sem.at[2]).wait()

    def wait_back(e):
        part = back.at[e, pl.ds(0, 16 * (NE - 1))]
        pltpu.make_async_copy(part, part, bk_s.at[e]).wait()
        pltpu.make_async_copy(part, part, bk_r.at[e]).wait()

    chunks = [("d", 0), ("d", 1), ("g", 0), ("u", 0), ("g", 1), ("u", 1)]

    def partial(m, quarter, half):
        kind, e = chunks[m]
        cols = pl.ds(pl.multiple_of(quarter * 512 + half * 256, 256), 256)
        a = (us if kind == "d" else xs)[e, :, cols]
        b = wh[e] if kind == "d" else dgu[e, 0 if kind == "g" else 1]
        return dot_tn(a, b)

    def sa_copy(m, d):
        return pltpu.make_async_remote_copy(
            src_ref=sa.at[m % 2, pl.ds(256 * d, 256)],
            dst_ref=ra.at[m, d],
            send_sem=sa_s.at[m, d],
            recv_sem=ra_r.at[m, d],
            device_id=((right, left)[d], me),
            device_id_type=MESH,
        )

    def sb_copy(m, d, h):
        rows = pl.ds(256 * h, 256)
        return pltpu.make_async_remote_copy(
            src_ref=sb.at[m % 2, d, rows],
            dst_ref=rb.at[m, d, rows],
            send_sem=sb_s.at[m, d, h],
            recv_sem=rb_r.at[m, d, h],
            device_id=((right, left)[d], me),
            device_id_type=MESH,
        )

    def step_a(m):
        for d in range(2):
            if m >= 2:
                sa_copy(m - 2, d).wait_send()
            sa[m % 2, 256 * d : 256 * d + 256, :] = partial(m, lax.rem(x + 2, NX), d).astype(BF)
            sa_copy(m, d).start()

    def step_b(m, h):
        for d in range(2):
            if m >= 2:
                sb_copy(m - 2, d, h).wait_send()
            total = partial(m, (right, left)[d], h)
            if h == d:
                sa_copy(m, d).wait_recv()
                total = total + ra[m, d].astype(F32)
            sb[m % 2, d, 256 * h : 256 * h + 256, :] = total.astype(BF)
            sb_copy(m, d, h).start()

    outs = {"d": gd, "g": gg, "u": gu}

    def out_copy(m):
        kind, e = chunks[m]
        return pltpu.make_async_copy(outd if kind == "d" else outv.at[m % 2], outs[kind].at[e], out_sem.at[m])

    def own_part(m):
        for h in range(2):
            own[256 * h : 256 * h + 256, :] = partial(m, x, h)

    def final(m):
        kind, e = chunks[m]
        own_part(m)
        if m == 1:
            out_copy(0).wait()
        if m >= 4:
            out_copy(m - 2).wait()
        for d in range(2):
            for h in range(2):
                sb_copy(m, d, h).wait_recv()
            pltpu.make_async_copy(rb.at[m, d], rbv.at[d], ld_sem.at[d]).start()
        for d in range(2):
            pltpu.make_async_copy(rb.at[m, d], rbv.at[d], ld_sem.at[d]).wait()

        def body(i, c):
            rows = pl.ds(pl.multiple_of(i * 128, 128), 128)
            total = own[rows, :] + rbv[0, rows, :].astype(F32) + rbv[1, rows, :].astype(F32)
            if kind == "d":
                outd[:, rows] = total.T.astype(BF)
            else:
                outv[m % 2, rows, :] = total.astype(BF)
            return c

        lax.fori_loop(0, 4, body, 0)
        out_copy(m).start()

    def combine():
        id_rows = ids[...].astype(F32).T.astype(jnp.int32)
        rank = slot_numbers(id_rows)
        dvals = jnp.zeros((128, 64), F32)
        for half in range(2):
            wait_back(half)
            loads = []
            for q in range(4):
                rows = pl.ds(128 * q, 128)
                for n, (at, w) in enumerate(((0, 1024), (1024, 1024), (D, 384))):
                    dst = stage.at[n // 2, n % 2, q // 2, q % 2, :, pl.ds(0, w)]
                    loads.append(pltpu.make_async_copy(back.at[half, rows, pl.ds(at, w)], dst, bk_l.at[q, n]))
            for load in loads:
                load.start()

            def held(n, at, w):
                return stage[n // 2, n % 2, 0:2, :, :, at : at + w].reshape(512, w)

            spread = jnp.where(iota((64, 512), 0) == 2 * (iota((64, 512), 1) // 16) + half, 1.0, 0.0).astype(BF)
            wide = dot(rank, spread)
            lane = iota((128, 512), 1) % 16
            pm = jnp.where(wide == (lane + 1).astype(F32), 1.0, 0.0).astype(BF)
            for load in loads:
                load.wait()
            for n in range(4):
                cols = slice(512 * n, 512 * n + 512)
                got = dot(pm, held(n // 2, 512 * (n % 2), 512))
                tokacc[:, cols] = got if half == 0 else tokacc[:, cols] + got
            over = held(2, 0, 256)
            info = held(2, 256, 128).astype(F32)
            own_expert = iota((512, 64), 1) == 2 * (iota((512, 64), 0) // 16) + half
            for q in range(8):
                po = jnp.where((wide == (17 + lane // 8).astype(F32)) & (lane % 8 == q), 1.0, 0.0).astype(BF)
                cols = slice(256 * q, 256 * q + 256)
                tokacc[:, cols] = tokacc[:, cols] + dot(po, over)
                if q == 0:
                    dvals = dvals + dot(po, jnp.where(own_expert, info[:, 1:2], 0.0).astype(BF))
            dvals = dvals + dot(pm, jnp.where(own_expert, info[:, 0:1], 0.0).astype(BF))
        gtok[...] = tokacc[...].astype(BF)
        expert = iota((128, 64), 1)
        picked = [
            jnp.sum(jnp.where(id_rows[:, k : k + 1] == expert, dvals, 0.0), axis=1, keepdims=True) for k in range(8)
        ]
        dgate = jnp.concatenate(picked, axis=1)
        dgate = dgate.T
        glog[...] = probs * (dgate - jnp.sum(probs * dgate, axis=0, keepdims=True))

    own_rows = [
        pltpu.make_async_copy(src, dxs.at[i, pl.ds(0, 128), pl.ds(0, D)], ld_sem.at[i])
        for i, src in enumerate((tokens, upstream))
    ]
    for cp in own_rows:
        cp.start()
    raised = jnp.exp(logits[...] - jnp.max(logits[...], axis=0, keepdims=True))
    probs = raised / jnp.sum(raised, axis=0, keepdims=True)
    meta[...] = jnp.concatenate([ids[...].astype(F32), probs.astype(BF).astype(F32)], axis=0).astype(BF)
    for cp in own_rows:
        cp.wait()
    pl.semaphore_wait(barrier, NE - 1 + 2)

    ag_own(0)
    share_routing()
    ag_ring(0)
    ag_chunk(0)
    ag_own(1)
    start_weights(0)
    wdload(0).start()
    read_routing()
    build_dispatch()
    fetch(0, 0)
    dispatch_tokens(0)
    ag_forward(0)
    fetch(0, 1)
    fetch(0, 2)
    ag_ring(1)
    dispatch_tokens(1)
    ag_chunk(1)
    dispatch_tokens(2)
    ag_own(2)
    ag_last(0)
    fetch(1, 0)
    fetch(0, 3)
    ag_forward(1)
    dispatch_tokens(3)
    fetch(1, 1)
    fetch(1, 2)
    ag_ring(2)
    forward(0, 0, 5)
    ag_chunk(2)
    ag_last(1)
    forward(0, 5, 9)
    fetch(1, 3)
    start_weights(1)
    dispatch_upstream(1)
    step_a(0)
    ag_own(3)
    ag_forward(2)
    forward(1, 0, 5)
    ag_ring(3)
    ag_last(2)
    forward(1, 5, 9)
    start_weights(0)
    step_a(1)
    ag_chunk(3)
    for n in range(4):
        fetch(2, n)
    dispatch_upstream(2)
    step_b(0, 0)
    ag_own(4)
    ag_forward(3)
    step_b(1, 0)
    ag_last(3)
    ag_ring(4)
    ag_chunk(4)
    for n in range(4):
        fetch(3, n)
    dispatch_upstream(3)
    step_b(0, 1)
    step_b(1, 1)
    ag_forward(4)
    ag_last(4)
    for n in range(4):
        fetch(4, n)
    dispatch_upstream(4)
    backward(0)
    step_a(2)
    for j in range(NJ):
        for r in range(2):
            for k in range(2):
                ag(j, r, k).wait_send()
    input_grad(0)
    start_weights(1)
    send_back(0)
    backward(1)
    step_b(2, 0)
    step_b(2, 1)
    step_a(3)
    input_grad(1)
    send_back(1)
    final(0)
    final(1)
    step_b(3, 0)
    step_b(3, 1)
    step_a(4)
    final(2)
    step_b(4, 0)
    step_b(4, 1)
    step_a(5)
    final(3)
    step_b(5, 0)
    step_b(5, 1)
    final(4)
    combine()
    final(5)
    for m in (4, 5):
        for d in range(2):
            sa_copy(m, d).wait_send()
            for h in range(2):
                sb_copy(m, d, h).wait_send()
    for m in (1, 4, 5):
        out_copy(m).wait()
    for j in range(NJ):
        for r in range(2):
            for k in range(2, 12):
                ag(j, r, k).wait_send()


def hand_over(*refs):
    src, dst, mid, sems = refs[0:5], refs[5:10], refs[10:15], refs[15]
    loads = [pltpu.make_async_copy(src[i], mid[i], sems.at[0, i]) for i in range(5)]
    stores = [pltpu.make_async_copy(mid[i], dst[i], sems.at[1, i]) for i in range(5)]
    for load in loads:
        load.start()
    for load, store in zip(loads, stores):
        load.wait()
        store.start()
    for store in stores:
        store.wait()


def on_device(tokens, expert_ids, gate_logits, upstream, w_gate, w_up, w_down):
    sd = jax.ShapeDtypeStruct
    dma = pltpu.SemaphoreType.DMA
    vm = pltpu.VMEM
    res = pl.pallas_call(
        kernel,
        out_shape=(
            sd((128, D), BF),
            sd((8, 128), F32),
            sd((2, 512, FF), BF),
            sd((2, 512, FF), BF),
            sd((2, FF, 512), BF),
            sd((6, 2, 512, FF), BF),
            sd((2, NE * 16, BACK), BF),
            *[sd((4, 4, 2, 128, w), BF) for w in JOBS for _ in range(2)],
        ),
        in_specs=[ANY] * 5 + [VMEM] * 2,
        out_specs=(VMEM, VMEM) + (ANY,) * 15,
        scratch_shapes=[
            vm((16, 128), BF),
            vm((NE, 16, 128), BF),
            vm((4, 16, 256), F32),
            vm((2, 2, 4, 2, 128, 1024), BF),
            vm((16, 80, 256), BF),
            vm((2, ROWS, D), BF),
            vm((2, ROWS, D), BF),
            vm((128, D + 128), F32),
            vm((2, ROWS, 128), F32),
            vm((D, FF), BF),
            vm((D, FF), BF),
            vm((FF, D), BF),
            vm((2, ROWS, FF), F32),
            vm((2, ROWS, FF), F32),
            vm((2, ROWS, FF), BF),
            vm((2, 2, ROWS, FF), BF),
            vm((ROWS, 128), F32),
            vm((2, 512, FF), BF),
            vm((6, 2, 256, FF), BF),
            vm((2, 2, 512, FF), BF),
            vm((2, 512, FF), BF),
            vm((512, FF), F32),
            vm((2, 512, FF), BF),
            vm((FF, 512), BF),
            vm((2, ROWS, BACK), BF),
            vm((128, D), F32),
            dma,
            dma,
            dma((NJ, 2, 12)),
            dma((NJ, 2, 12)),
            dma((NJ, 2)),
            dma((2, 2, 4)),
            dma((3,)),
            dma((6, 2)),
            dma((6, 2)),
            dma((6, 2, 2)),
            dma((6, 2, 2)),
            dma((2,)),
            dma((2,)),
            dma((4, 3)),
            dma((4,)),
            dma((6,)),
        ],
        compiler_params=pltpu.CompilerParams(collective_id=0, has_side_effects=True, vmem_limit_bytes=64 << 20),
        cost_estimate=pl.CostEstimate(flops=29 * 10**9, bytes_accessed=10**8, transcendentals=10**6),
        name="expert_backward",
    )(tokens, upstream, w_gate, w_up, w_down, expert_ids.T, gate_logits.T)
    done = pl.pallas_call(
        hand_over,
        out_shape=tuple(sd(r.shape, r.dtype) for r in res[:5]),
        in_specs=[ANY] * 5,
        out_specs=(ANY,) * 5,
        scratch_shapes=[vm(r.shape, r.dtype) for r in res[:5]] + [dma((2, 5))],
        name="hand_over",
    )(*res[:5])
    return (done[0], done[1].T) + tuple(done[2:])


def solution(mesh):
    rows = P(("dp", "expert"), None)
    whole = P("expert", None, None)
    return jax.shard_map(
        on_device,
        mesh=mesh,
        in_specs=(rows, rows, rows, rows, whole, whole, whole),
        out_specs=(rows, rows, P("expert", "dp", None), P("expert", "dp", None), P("expert", None, "dp")),
        check_vma=False,
    )
```

```python
import jax
import jax.numpy as jnp
from jax import lax
from jax.experimental import pallas as pl
from jax.experimental.pallas import tpu as pltpu
from jax.sharding import PartitionSpec as P

MESH = pl.DeviceIdType.MESH
BF = jnp.bfloat16
F32 = jnp.float32
D, FF, NE, NX = 2048, 768, 32, 4
MAIN, OVF = 16, 2
ROWS = NE * (MAIN + OVF)
BACK = D + 256 + 128
ANY = pl.BlockSpec(memory_space=pl.ANY)
VMEM = pl.BlockSpec(memory_space=pltpu.VMEM)


def iota(shape, dim):
    return lax.broadcasted_iota(jnp.int32, shape, dim)


def dot_nt(a, b):
    return lax.dot_general(a, b, (((1,), (1,)), ((), ())), preferred_element_type=F32)


def dot_tn(a, b):
    return lax.dot_general(a, b, (((0,), (0,)), ((), ())), preferred_element_type=F32)


def dot(a, b):
    return jnp.dot(a, b, preferred_element_type=F32)


def slot_numbers(ids):
    expert = iota((128, 64), 1)
    routed = jnp.zeros((128, 64), F32)
    for k in range(8):
        routed = routed + jnp.where(ids[:, k : k + 1] == expert, 1.0, 0.0)
    before = jnp.where(iota((128, 128), 1) < iota((128, 128), 0), 1.0, 0.0)
    rank = dot(before.astype(BF), routed.astype(BF))
    return jnp.where(routed > 0, rank + 1.0, 0.0).astype(BF)


def slot_targets():
    row, lane = iota((80, 256), 0), iota((80, 256), 1)
    over = row - 64
    core = jnp.where(row < 64, (row % 32) // 16, (over % 4) // 2)
    slot = jnp.where(row < 64, row % 16, 16 + over % 2)
    ok = (core == lane // 128) & (row < 72)
    second = ((row >= 32) & (row < 64)) | (over >= 4)
    return jnp.where(ok, slot + 1, -1).astype(F32), jnp.where(second, 1.0, 0.0)


JOBS = (1024, 256, 256, 256, 256)
NJ = len(JOBS)


def kernel(
    tokens, upstream, wg, wu, wd, ids, logits,
    gtok, glog, gg, gu, gd, rb, back, g00, g01, g10, g11, g20, g21, g30, g31, g40, g41,
    meta, metas, ranks, stage, pmat, xs, us, ov, xgate, wgv, wuv, wdv, pre_g, pre_u, wh, dgu, dgacc,
    sa, ra, sb, rbv, own, outv, outd, dxs, tokacc,
    mt_s, mt_r, ag_s, ag_r, ag_l, stage_sem, w_sem, sa_s, ra_r, sb_s, rb_r, bk_s, bk_r, bk_l, ld_sem, out_sem,
):
    gathered = ((g00, g01), (g10, g11), (g20, g21), (g30, g31), (g40, g41))
    x, me = lax.axis_index("dp"), lax.axis_index("expert")
    right, left = lax.rem(x + 1, NX), lax.rem(x + 3, NX)
    z, y, core = me // 8, (me // 2) % 4, me % 2

    barrier = pltpu.get_barrier_semaphore()

    def greet(i, c):
        pl.semaphore_signal(barrier, inc=1, device_id=(x, lax.rem(me + i, NE)), device_id_type=MESH)
        return c

    lax.fori_loop(1, NE, greet, 0)
    for other in (right, left):
        pl.semaphore_signal(barrier, inc=1, device_id=(other, me), device_id_type=MESH)

    def wload(e):
        return [
            pltpu.make_async_copy(wg.at[e], wgv, w_sem.at[0]),
            pltpu.make_async_copy(wu.at[e], wuv, w_sem.at[1]),
        ]

    def wdload(e):
        return pltpu.make_async_copy(wd.at[e], wdv, w_sem.at[2])

    def start_weights(e):
        for cp in wload(e):
            cp.start()

    def place(r, a, b):
        return (b, a) if r == 0 else (a, b)

    def peer(r, a, b):
        pz, py = place(r, a % 4, b % 4)
        return (pz * 4 + py) * 2 + core

    pos = ((y, z), (z, y))

    def chunk(j, r, b, half=None):
        g = gathered[j][r]
        span = pl.ds(0, 4) if half is None else pl.ds(2 * half, 2)
        return g.at[b % 4, span, core] if r == 0 else g.at[span, b % 4, core]

    def block(j, r, a):
        pz, py = place(r, a % 4, pos[r][1])
        return gathered[j][r].at[pz, py, core]

    def column(j, r):
        if j == 0:
            return 1024 * r
        quarter = (lax.rem(x + 2, NX), (right, left)[r], (right, left)[r], x)[j - 1]
        return pl.multiple_of(512 * quarter + (256 * r, 0, 256, 256 * r)[j - 1], 256)

    def source(j, r):
        return dxs.at[min(j, 1), pl.ds(0, 128), pl.ds(column(j, r), JOBS[j])]

    def ag(j, r, k):
        p1, p2 = pos[r]
        if k < 2:
            src, dst = source(j, r), block(j, r, p1)
        elif k < 4:
            rows = pl.ds(64 * (k - 2), 64)
            src = dst = block(j, r, p1 + (3, 1)[k - 2]).at[rows]
        elif k < 6:
            src = dst = chunk(j, r, p2)
        elif k < 8:
            src = dst = chunk(j, r, p2 + (3, 1)[k - 6], half=k - 6)
        else:
            src = dst = chunk(j, r, p2 + (0, 3, 1, 2)[k - 8])
        if k < 4:
            to = peer(r, p1 + (1, 3)[k % 2], p2)
        elif k < 8:
            to = peer(r, p1, p2 + (1, 3)[k % 2])
        else:
            to = (z * 4 + y) * 2 + 1 - core
        return pltpu.make_async_remote_copy(
            src_ref=src,
            dst_ref=dst,
            send_sem=ag_s.at[j, r, k],
            recv_sem=ag_r.at[j, r, k],
            device_id=(x, to),
            device_id_type=MESH,
        )

    def keep(j, r):
        return pltpu.make_async_copy(source(j, r), block(j, r, pos[r][0]), ag_l.at[j, r])

    def ag_own(j):
        for r in range(2):
            ag(j, r, 0).start()
            ag(j, r, 1).start()
            keep(j, r).start()

    def ag_ring(j):
        for r in range(2):
            for k in range(2):
                ag(j, r, k).wait_recv()
                ag(j, r, k + 2).start()

    def ag_chunk(j):
        for r in range(2):
            ag(j, r, 2).wait_recv()
            ag(j, r, 3).wait_recv()
            keep(j, r).wait()
            for k in (4, 5, 8):
                ag(j, r, k).start()

    def ag_forward(j):
        for r in range(2):
            for k in range(2):
                ag(j, r, k + 4).wait_recv()
                ag(j, r, k + 6).start()
                ag(j, r, k + 9).start()

    def ag_last(j):
        for r in range(2):
            ag(j, r, 6).wait_recv()
            ag(j, r, 7).wait_recv()
            ag(j, r, 11).start()

    target, second = slot_targets()

    def order(r, n):
        return (pos[r][1] + (0, 3, 1, 2)[n]) % 4

    def load(j, r, n):
        g = gathered[j][r]
        b = order(r, n)
        part = (n % 2, 0, 1024) if j == 0 else ((j - 1) % 2, 256 * n, 256)
        src = g.at[b] if r == 0 else g.at[:, b]
        return pltpu.make_async_copy(
            src, stage.at[part[0], r, :, :, :, pl.ds(part[1], part[2])], stage_sem.at[part[0], r, 0 if j == 0 else n]
        )

    def fetch(j, n):
        for r in range(2):
            ag(j, r, 8 + n).wait_recv()
            load(j, r, n).start()

    def multiply(j, r, b, k, half, strip):
        dst = xs if j == 0 else us
        base = column(j, r)
        pz, py = place(r, k, b)
        chip = pz * 4 + py
        at = pl.multiple_of(32 * chip, 32)
        w = 512 if j == 0 else 256
        pm = pmat[chip]
        for off in range(0, JOBS[j], w):
            got = dot(pm, stage[half, r, k, :, :, pl.ds(strip + off, w)].reshape(256, w))
            cols = pl.ds(base + off, w)
            dst[0, pl.ds(at, 32), cols] = got[0:32].astype(BF)
            dst[1, pl.ds(at, 32), cols] = got[32:64].astype(BF)
            ov[pl.ds(pl.multiple_of(8 * chip, 8), 8), cols] = got[64:72]

    def dispatch_tokens(n):
        for r in range(2):
            load(0, r, n).wait()

            def body(k, c, r=r):
                multiply(0, r, order(r, n), k, n % 2, 0)
                return c

            lax.fori_loop(0, 4, body, 0)
        if n == 3:
            overflow(0, 0)
            overflow(0, 1)

    def dispatch_upstream(j):
        for r in range(2):
            for n in range(4):
                load(j, r, n).wait()

                def body(k, c, r=r, n=n):
                    multiply(j, r, order(r, n), k, (j - 1) % 2, 256 * n)
                    return c

                lax.fori_loop(0, 4, body, 0)
            overflow(j, r)

    def overflow(j, r):
        dst = xs if j == 0 else us
        row, col = iota((64, 128), 0), iota((64, 128), 1)
        w = 512 if j == 0 else 256
        for e in range(2):
            sel = jnp.where(col == 8 * (row // 4) + 4 * e + row % 4, 1.0, 0.0).astype(BF)
            for off in range(0, JOBS[j], w):
                cols = pl.ds(column(j, r) + off, w)
                dst[e, 512:576, cols] = dot(sel, ov[:, cols].astype(BF)).astype(BF)

    def share_routing():
        def body(i, c):
            p = lax.rem(me + i, NE)
            pltpu.make_async_remote_copy(
                src_ref=meta,
                dst_ref=metas.at[me],
                send_sem=mt_s,
                recv_sem=mt_r,
                device_id=(x, p),
                device_id_type=MESH,
            ).start()
            return c

        lax.fori_loop(1, NE, body, 0)

    def read_routing():
        metas[me] = meta[...]
        part = metas.at[pl.ds(0, NE - 1)]
        pltpu.make_async_copy(part, part, mt_s).wait()
        pltpu.make_async_copy(part, part, mt_r).wait()
        known = metas[...].astype(F32)
        before = jnp.where(iota((128, 128), 0) < iota((128, 128), 1), 1.0, 0.0).astype(BF)
        for e in range(2):
            hit = jnp.where(known[:, 0:8, :] == (2 * me + e).astype(F32), 1.0, 0.0)
            routed = jnp.sum(hit, axis=1)
            gates = jnp.sum(hit * known[:, 8:16, :], axis=1)
            number = jnp.where(routed > 0, dot(routed.astype(BF), before) + 1.0, 0.0)
            for h in range(2):
                pick = jnp.where(iota((16, NE), 1) == 2 * iota((16, NE), 0) + h, 1.0, 0.0).astype(BF)
                ranks[e, :, 128 * h : 128 * h + 128] = dot(pick, number.astype(BF))
                ranks[2 + e, :, 128 * h : 128 * h + 128] = dot(pick, gates.astype(BF))

    def build_dispatch():
        def body(chip, c):
            at = pl.multiple_of(32 * chip, 32)

            def rows(n):
                pair = [jnp.broadcast_to(ranks[n + e, pl.ds(chip, 1), :], (80, 256)) for e in range(2)]
                return jnp.where(second > 0.5, pair[1], pair[0])

            pm = jnp.where(rows(0) == target, 1.0, 0.0)
            pmat[chip] = pm.astype(BF)
            got = jnp.broadcast_to(jnp.sum(pm * rows(2), axis=1, keepdims=True), (80, 128))
            xgate[0, pl.ds(at, 32), :] = got[0:32]
            xgate[1, pl.ds(at, 32), :] = got[32:64]
            ov[pl.ds(pl.multiple_of(8 * chip, 8), 8), D : D + 128] = got[64:72]
            return c

        lax.fori_loop(0, 16, body, 0)
        row, col = iota((64, 128), 0), iota((64, 128), 1)
        for e in range(2):
            sel = jnp.where(col == 8 * (row // 4) + 4 * e + row % 4, 1.0, 0.0).astype(BF)
            xgate[e, 512:576, :] = dot(sel, ov[:, D : D + 128].astype(BF))

    def gate_of(e, rows):
        return xgate[e, rows, 0:1]

    def forward(e, lo, hi):
        if lo == 0:
            for cp in wload(e):
                cp.wait()

        def body(i, c):
            rows = pl.ds(pl.multiple_of((i // 3) * 192, 192), 192)
            cols = pl.ds(pl.multiple_of((i % 3) * 256, 256), 256)
            pg = dot(xs[e, rows, :], wgv[:, cols])
            pu = dot(xs[e, rows, :], wuv[:, cols])
            pre_g[e, rows, cols] = pg
            pre_u[e, rows, cols] = pu
            hidden = pg * jax.nn.sigmoid(pg) * pu
            wh[e, rows, cols] = (gate_of(e, rows) * hidden).astype(BF)
            return c

        lax.fori_loop(lo, hi, body, 0)

    def backward(e):
        wdload(e).wait()

        def body(i, c):
            rows = pl.ds(pl.multiple_of((i // 3) * 192, 192), 192)
            cols = pl.ds(pl.multiple_of((i % 3) * 256, 256), 256)
            raw = dot_nt(us[e, rows, :], wdv[cols, :])
            pg, pu = pre_g[e, rows, cols], pre_u[e, rows, cols]
            s = jax.nn.sigmoid(pg)
            act = pg * s
            part = raw * (act * pu)
            part = part[:, 0:128] + part[:, 128:256]
            dgacc[rows, :] = jnp.where(i % 3 == 0, jnp.zeros_like(part), dgacc[rows, :]) + part
            dh = gate_of(e, rows) * raw
            dgu[e, 0, rows, cols] = (dh * pu * s * (1.0 + pg * (1.0 - s))).astype(BF)
            dgu[e, 1, rows, cols] = (dh * act).astype(BF)
            return c

        lax.fori_loop(0, 9, body, 0)
        if e == 0:
            wdload(1).start()

    def input_grad(e):
        for cp in wload(e):
            cp.wait()

        def body(i, c):
            rows = pl.ds(pl.multiple_of((i // 4) * 192, 192), 192)
            cols = pl.ds(pl.multiple_of((i % 4) * 512, 512), 512)
            dx = dot_nt(dgu[e, 0, rows, :], wgv[cols, :]) + dot_nt(dgu[e, 1, rows, :], wuv[cols, :])
            dxs[e, rows, cols] = dx.astype(BF)
            return c

        lax.fori_loop(0, 12, body, 0)
        r, col = iota((512, 64), 0), iota((512, 64), 1)
        place = 2 * (r // 16) + (r % 16) // 8 == col
        packed = jnp.zeros((512, 256), F32)
        for q in range(8):
            sel = jnp.where(place & (r % 8 == q), 1.0, 0.0).astype(BF)
            packed = packed + dot(sel, dxs[e, 512:576, 256 * q : 256 * q + 256])
        dxs[e, 0:512, D : D + 256] = packed.astype(BF)
        dgate = jnp.sum(dgacc[...], axis=1, keepdims=True).astype(BF).astype(F32)
        first = iota((512, 128), 1) == 0
        sel = jnp.where(place & (r % 8 == 0), 1.0, 0.0).astype(BF)
        over = dot(sel, jnp.broadcast_to(dgate[512:576], (64, 128)).astype(BF))
        main = jnp.broadcast_to(dgate[0:512], (512, 128))
        dxs[e, 0:512, D + 256 :] = jnp.where(first, main, over).astype(BF)

    def send_back(e):
        pltpu.make_async_copy(dxs.at[e, pl.ds(pl.multiple_of(16 * me, 16), 16)], back.at[e, pl.ds(pl.multiple_of(16 * me, 16), 16)], ld_sem.at[2]).start()

        def body(i, c):
            p = lax.rem(me + i, NE)
            pltpu.make_async_remote_copy(
                src_ref=dxs.at[e, pl.ds(pl.multiple_of(16 * p, 16), 16)],
                dst_ref=back.at[e, pl.ds(pl.multiple_of(16 * me, 16), 16)],
                send_sem=bk_s.at[e],
                recv_sem=bk_r.at[e],
                device_id=(x, p),
                device_id_type=MESH,
            ).start()
            return c

        lax.fori_loop(1, NE, body, 0)
        pltpu.make_async_copy(dxs.at[e, pl.ds(pl.multiple_of(16 * me, 16), 16)], back.at[e, pl.ds(pl.multiple_of(16 * me, 16), 16)], ld_sem.at[2]).wait()

    def wait_back(e):
        part = back.at[e, pl.ds(0, 16 * (NE - 1))]
        pltpu.make_async_copy(part, part, bk_s.at[e]).wait()
        pltpu.make_async_copy(part, part, bk_r.at[e]).wait()

    chunks = [("d", 0), ("d", 1), ("g", 0), ("u", 0), ("g", 1), ("u", 1)]

    def partial(m, quarter, half):
        kind, e = chunks[m]
        cols = pl.ds(pl.multiple_of(quarter * 512 + half * 256, 256), 256)
        a = (us if kind == "d" else xs)[e, :, cols]
        b = wh[e] if kind == "d" else dgu[e, 0 if kind == "g" else 1]
        return dot_tn(a, b)

    def sa_copy(m, d):
        return pltpu.make_async_remote_copy(
            src_ref=sa.at[m % 2, pl.ds(256 * d, 256)],
            dst_ref=ra.at[m, d],
            send_sem=sa_s.at[m, d],
            recv_sem=ra_r.at[m, d],
            device_id=((right, left)[d], me),
            device_id_type=MESH,
        )

    def sb_copy(m, d, h):
        rows = pl.ds(256 * h, 256)
        return pltpu.make_async_remote_copy(
            src_ref=sb.at[m % 2, d, rows],
            dst_ref=rb.at[m, d, rows],
            send_sem=sb_s.at[m, d, h],
            recv_sem=rb_r.at[m, d, h],
            device_id=((right, left)[d], me),
            device_id_type=MESH,
        )

    def step_a(m):
        for d in range(2):
            if m >= 2:
                sa_copy(m - 2, d).wait_send()
            sa[m % 2, 256 * d : 256 * d + 256, :] = partial(m, lax.rem(x + 2, NX), d).astype(BF)
            sa_copy(m, d).start()

    def step_b(m, h):
        for d in range(2):
            if m >= 2:
                sb_copy(m - 2, d, h).wait_send()
            total = partial(m, (right, left)[d], h)
            if h == d:
                sa_copy(m, d).wait_recv()
                total = total + ra[m, d].astype(F32)
            sb[m % 2, d, 256 * h : 256 * h + 256, :] = total.astype(BF)
            sb_copy(m, d, h).start()

    outs = {"d": gd, "g": gg, "u": gu}

    def out_copy(m):
        kind, e = chunks[m]
        return pltpu.make_async_copy(outd if kind == "d" else outv.at[m % 2], outs[kind].at[e], out_sem.at[m])

    def own_part(m):
        for h in range(2):
            own[256 * h : 256 * h + 256, :] = partial(m, x, h)

    def final(m):
        kind, e = chunks[m]
        own_part(m)
        if m == 1:
            out_copy(0).wait()
        if m >= 4:
            out_copy(m - 2).wait()
        for d in range(2):
            for h in range(2):
                sb_copy(m, d, h).wait_recv()
            pltpu.make_async_copy(rb.at[m, d], rbv.at[d], ld_sem.at[d]).start()
        for d in range(2):
            pltpu.make_async_copy(rb.at[m, d], rbv.at[d], ld_sem.at[d]).wait()

        def body(i, c):
            rows = pl.ds(pl.multiple_of(i * 128, 128), 128)
            total = own[rows, :] + rbv[0, rows, :].astype(F32) + rbv[1, rows, :].astype(F32)
            if kind == "d":
                outd[:, rows] = total.T.astype(BF)
            else:
                outv[m % 2, rows, :] = total.astype(BF)
            return c

        lax.fori_loop(0, 4, body, 0)
        out_copy(m).start()

    def combine():
        id_rows = ids[...].astype(F32).T.astype(jnp.int32)
        rank = slot_numbers(id_rows)
        dvals = jnp.zeros((128, 64), F32)
        for half in range(2):
            wait_back(half)
            loads = []
            for q in range(4):
                rows = pl.ds(128 * q, 128)
                for n, (at, w) in enumerate(((0, 1024), (1024, 1024), (D, 384))):
                    dst = stage.at[n // 2, n % 2, q // 2, q % 2, :, pl.ds(0, w)]
                    loads.append(pltpu.make_async_copy(back.at[half, rows, pl.ds(at, w)], dst, bk_l.at[q, n]))
            for load in loads:
                load.start()

            def held(n, at, w):
                return stage[n // 2, n % 2, 0:2, :, :, at : at + w].reshape(512, w)

            spread = jnp.where(iota((64, 512), 0) == 2 * (iota((64, 512), 1) // 16) + half, 1.0, 0.0).astype(BF)
            wide = dot(rank, spread)
            lane = iota((128, 512), 1) % 16
            pm = jnp.where(wide == (lane + 1).astype(F32), 1.0, 0.0).astype(BF)
            for load in loads:
                load.wait()
            for n in range(4):
                cols = slice(512 * n, 512 * n + 512)
                got = dot(pm, held(n // 2, 512 * (n % 2), 512))
                tokacc[:, cols] = got if half == 0 else tokacc[:, cols] + got
            over = held(2, 0, 256)
            info = held(2, 256, 128).astype(F32)
            own_expert = iota((512, 64), 1) == 2 * (iota((512, 64), 0) // 16) + half
            for q in range(8):
                po = jnp.where((wide == (17 + lane // 8).astype(F32)) & (lane % 8 == q), 1.0, 0.0).astype(BF)
                cols = slice(256 * q, 256 * q + 256)
                tokacc[:, cols] = tokacc[:, cols] + dot(po, over)
                if q == 0:
                    dvals = dvals + dot(po, jnp.where(own_expert, info[:, 1:2], 0.0).astype(BF))
            dvals = dvals + dot(pm, jnp.where(own_expert, info[:, 0:1], 0.0).astype(BF))
        gtok[...] = tokacc[...].astype(BF)
        expert = iota((128, 64), 1)
        picked = [
            jnp.sum(jnp.where(id_rows[:, k : k + 1] == expert, dvals, 0.0), axis=1, keepdims=True) for k in range(8)
        ]
        dgate = jnp.concatenate(picked, axis=1)
        dgate = dgate.T
        glog[...] = probs * (dgate - jnp.sum(probs * dgate, axis=0, keepdims=True))

    own_rows = [
        pltpu.make_async_copy(src, dxs.at[i, pl.ds(0, 128), pl.ds(0, D)], ld_sem.at[i])
        for i, src in enumerate((tokens, upstream))
    ]
    for cp in own_rows:
        cp.start()
    raised = jnp.exp(logits[...] - jnp.max(logits[...], axis=0, keepdims=True))
    probs = raised / jnp.sum(raised, axis=0, keepdims=True)
    meta[...] = jnp.concatenate([ids[...].astype(F32), probs.astype(BF).astype(F32)], axis=0).astype(BF)
    for cp in own_rows:
        cp.wait()
    pl.semaphore_wait(barrier, NE - 1 + 2)

    ag_own(0)
    share_routing()
    ag_ring(0)
    ag_chunk(0)
    ag_own(1)
    start_weights(0)
    wdload(0).start()
    read_routing()
    build_dispatch()
    fetch(0, 0)
    dispatch_tokens(0)
    ag_forward(0)
    fetch(0, 1)
    fetch(0, 2)
    ag_ring(1)
    dispatch_tokens(1)
    ag_chunk(1)
    dispatch_tokens(2)
    ag_own(2)
    ag_last(0)
    fetch(1, 0)
    fetch(0, 3)
    ag_forward(1)
    dispatch_tokens(3)
    fetch(1, 1)
    fetch(1, 2)
    ag_ring(2)
    forward(0, 0, 5)
    ag_chunk(2)
    ag_last(1)
    forward(0, 5, 9)
    fetch(1, 3)
    start_weights(1)
    dispatch_upstream(1)
    step_a(0)
    ag_own(3)
    ag_forward(2)
    forward(1, 0, 5)
    ag_ring(3)
    ag_last(2)
    forward(1, 5, 9)
    start_weights(0)
    step_a(1)
    ag_chunk(3)
    ag_own(4)
    for n in range(4):
        fetch(2, n)
    dispatch_upstream(2)
    ag_ring(4)
    ag_forward(3)
    step_b(0, 0)
    ag_chunk(4)
    ag_last(3)
    step_b(1, 0)
    for n in range(4):
        fetch(3, n)
    dispatch_upstream(3)
    ag_forward(4)
    step_b(0, 1)
    ag_last(4)
    step_b(1, 1)
    for n in range(4):
        fetch(4, n)
    dispatch_upstream(4)
    backward(0)
    step_a(2)
    step_a(3)
    for j in range(NJ):
        for r in range(2):
            for k in range(2):
                ag(j, r, k).wait_send()
    input_grad(0)
    start_weights(1)
    send_back(0)
    step_b(2, 0)
    step_b(2, 1)
    backward(1)
    input_grad(1)
    send_back(1)
    step_b(3, 0)
    step_b(3, 1)
    step_a(4)
    step_a(5)
    final(0)
    final(1)
    final(2)
    step_b(4, 0)
    step_b(4, 1)
    final(3)
    step_b(5, 0)
    step_b(5, 1)
    final(4)
    combine()
    final(5)
    for m in (4, 5):
        for d in range(2):
            sa_copy(m, d).wait_send()
            for h in range(2):
                sb_copy(m, d, h).wait_send()
    for m in (1, 4, 5):
        out_copy(m).wait()
    for j in range(NJ):
        for r in range(2):
            for k in range(2, 12):
                ag(j, r, k).wait_send()


def hand_over(*refs):
    src, dst, mid, sems = refs[0:5], refs[5:10], refs[10:15], refs[15]
    loads = [pltpu.make_async_copy(src[i], mid[i], sems.at[0, i]) for i in range(5)]
    stores = [pltpu.make_async_copy(mid[i], dst[i], sems.at[1, i]) for i in range(5)]
    for load in loads:
        load.start()
    for load, store in zip(loads, stores):
        load.wait()
        store.start()
    for store in stores:
        store.wait()


def on_device(tokens, expert_ids, gate_logits, upstream, w_gate, w_up, w_down):
    sd = jax.ShapeDtypeStruct
    dma = pltpu.SemaphoreType.DMA
    vm = pltpu.VMEM
    res = pl.pallas_call(
        kernel,
        out_shape=(
            sd((128, D), BF),
            sd((8, 128), F32),
            sd((2, 512, FF), BF),
            sd((2, 512, FF), BF),
            sd((2, FF, 512), BF),
            sd((6, 2, 512, FF), BF),
            sd((2, NE * 16, BACK), BF),
            *[sd((4, 4, 2, 128, w), BF) for w in JOBS for _ in range(2)],
        ),
        in_specs=[ANY] * 5 + [VMEM] * 2,
        out_specs=(VMEM, VMEM) + (ANY,) * 15,
        scratch_shapes=[
            vm((16, 128), BF),
            vm((NE, 16, 128), BF),
            vm((4, 16, 256), F32),
            vm((2, 2, 4, 2, 128, 1024), BF),
            vm((16, 80, 256), BF),
            vm((2, ROWS, D), BF),
            vm((2, ROWS, D), BF),
            vm((128, D + 128), F32),
            vm((2, ROWS, 128), F32),
            vm((D, FF), BF),
            vm((D, FF), BF),
            vm((FF, D), BF),
            vm((2, ROWS, FF), F32),
            vm((2, ROWS, FF), F32),
            vm((2, ROWS, FF), BF),
            vm((2, 2, ROWS, FF), BF),
            vm((ROWS, 128), F32),
            vm((2, 512, FF), BF),
            vm((6, 2, 256, FF), BF),
            vm((2, 2, 512, FF), BF),
            vm((2, 512, FF), BF),
            vm((512, FF), F32),
            vm((2, 512, FF), BF),
            vm((FF, 512), BF),
            vm((2, ROWS, BACK), BF),
            vm((128, D), F32),
            dma,
            dma,
            dma((NJ, 2, 12)),
            dma((NJ, 2, 12)),
            dma((NJ, 2)),
            dma((2, 2, 4)),
            dma((3,)),
            dma((6, 2)),
            dma((6, 2)),
            dma((6, 2, 2)),
            dma((6, 2, 2)),
            dma((2,)),
            dma((2,)),
            dma((4, 3)),
            dma((4,)),
            dma((6,)),
        ],
        compiler_params=pltpu.CompilerParams(collective_id=0, has_side_effects=True, vmem_limit_bytes=64 << 20),
        cost_estimate=pl.CostEstimate(flops=29 * 10**9, bytes_accessed=10**8, transcendentals=10**6),
        name="expert_backward",
    )(tokens, upstream, w_gate, w_up, w_down, expert_ids.T, gate_logits.T)
    done = pl.pallas_call(
        hand_over,
        out_shape=tuple(sd(r.shape, r.dtype) for r in res[:5]),
        in_specs=[ANY] * 5,
        out_specs=(ANY,) * 5,
        scratch_shapes=[vm(r.shape, r.dtype) for r in res[:5]] + [dma((2, 5))],
        name="hand_over",
    )(*res[:5])
    return (done[0], done[1].T) + tuple(done[2:])


def solution(mesh):
    rows = P(("dp", "expert"), None)
    whole = P("expert", None, None)
    return jax.shard_map(
        on_device,
        mesh=mesh,
        in_specs=(rows, rows, rows, rows, whole, whole, whole),
        out_specs=(rows, rows, P("expert", "dp", None), P("expert", "dp", None), P("expert", None, "dp")),
        check_vma=False,
    )
```
